128 devices in a mesh: ctx: 8 (over x, z_lo), fsdp: 16 (over z_hi, y, core).
Axes of the slice: x: 4, y: 4, z: 4 (z_hi: 2, z_lo: 2; z = z_hi * 2 + z_lo), core: 2. Of those that a mesh axis runs over, the one named last changes fastest.
Arguments:
- hidden_in: bfloat16 [16, 1024, 2048], P('fsdp', 'ctx'), may hold values from -6 to 6
- cotangent: bfloat16 [16, 1024, 2048], P('fsdp', 'ctx'), may hold values from -6 to 6
- block_table: int32 [16, 16], P('fsdp'), may hold values from 0 to 15, as said below
- positions: int32 [16, 1024], P('fsdp', 'ctx'), may hold values from 0 to 2047, as said below
- query_weight: float32 [1, 2048, 2048], P(None, ('ctx', 'fsdp')), may hold values from -0.125 to 0.125
- key_weight: float32 [1, 2048, 256], P(None, ('ctx', 'fsdp')), may hold values from -0.125 to 0.125
- value_weight: float32 [1, 2048, 256], P(None, ('ctx', 'fsdp')), may hold values from -0.125 to 0.125
- output_weight: float32 [1, 2048, 2048], P(None, ('ctx', 'fsdp')), may hold values from -2 to 2
- gate_weight: float32 [1, 5632, 2048], P(None, ('ctx', 'fsdp')), may hold values from -0.125 to 0.125
- up_weight: float32 [1, 5632, 2048], P(None, ('ctx', 'fsdp')), may hold values from -0.125 to 0.125
- down_weight: float32 [1, 5632, 2048], P(None, ('ctx', 'fsdp')), may hold values from -0.078125 to 0.078125
- norm_gains: float32 [1, 2048, 2], P(None, ('ctx', 'fsdp')), may hold values from 0.5 to 1.5
- query_first: float32 [1, 2048, 2048], P(None, ('ctx', 'fsdp')), may hold values from -80 to 80
- key_first: float32 [1, 2048, 256], P(None, ('ctx', 'fsdp')), may hold values from -256 to 256
- value_first: float32 [1, 2048, 256], P(None, ('ctx', 'fsdp')), may hold values from -256 to 256
- output_first: float32 [1, 2048, 2048], P(None, ('ctx', 'fsdp')), may hold values from -6 to 6
- gate_first: float32 [1, 5632, 2048], P(None, ('ctx', 'fsdp')), may hold values from -32 to 32
- up_first: float32 [1, 5632, 2048], P(None, ('ctx', 'fsdp')), may hold values from -32 to 32
- down_first: float32 [1, 5632, 2048], P(None, ('ctx', 'fsdp')), may hold values from -48 to 48
- gains_first: float32 [1, 2048, 2], P(None, ('ctx', 'fsdp')), may hold values from -128 to 128
- query_second: float32 [1, 2048, 2048], P(None, ('ctx', 'fsdp')), may hold values from 425.984 to 6881.28
- key_second: float32 [1, 2048, 256], P(None, ('ctx', 'fsdp')), may hold values from 3932.16 to 62259.2
- value_second: float32 [1, 2048, 256], P(None, ('ctx', 'fsdp')), may hold values from 3932.16 to 62259.2
- output_second: float32 [1, 2048, 2048], P(None, ('ctx', 'fsdp')), may hold values from 1.6 to 27.2
- gate_second: float32 [1, 5632, 2048], P(None, ('ctx', 'fsdp')), may hold values from 52.4288 to 835.584
- up_second: float32 [1, 5632, 2048], P(None, ('ctx', 'fsdp')), may hold values from 52.4288 to 835.584
- down_second: float32 [1, 5632, 2048], P(None, ('ctx', 'fsdp')), may hold values from 154.0096 to 2457.6
- gains_second: float32 [1, 2048, 2], P(None, ('ctx', 'fsdp')), may hold values from 966.656 to 15564.8
Outputs:
- hidden_out: bfloat16 [16, 1024, 2048], P('fsdp', 'ctx')
- hidden_grad: float32 [16, 1024, 2048], P('fsdp', 'ctx')
- query_grad: float32 [1, 2048, 2048], P(None, ('ctx', 'fsdp'))
- query_update: float32 [1, 2048, 2048], P(None, ('ctx', 'fsdp'))
- query_momentum: float32 [1, 2048, 2048], P(None, ('ctx', 'fsdp'))
- query_variance: float32 [1, 2048, 2048], P(None, ('ctx', 'fsdp'))
- key_grad: float32 [1, 2048, 256], P(None, ('ctx', 'fsdp'))
- key_update: float32 [1, 2048, 256], P(None, ('ctx', 'fsdp'))
- key_momentum: float32 [1, 2048, 256], P(None, ('ctx', 'fsdp'))
- key_variance: float32 [1, 2048, 256], P(None, ('ctx', 'fsdp'))
- value_grad: float32 [1, 2048, 256], P(None, ('ctx', 'fsdp'))
- value_update: float32 [1, 2048, 256], P(None, ('ctx', 'fsdp'))
- value_momentum: float32 [1, 2048, 256], P(None, ('ctx', 'fsdp'))
- value_variance: float32 [1, 2048, 256], P(None, ('ctx', 'fsdp'))
- output_grad: float32 [1, 2048, 2048], P(None, ('ctx', 'fsdp'))
- output_update: float32 [1, 2048, 2048], P(None, ('ctx', 'fsdp'))
- output_momentum: float32 [1, 2048, 2048], P(None, ('ctx', 'fsdp'))
- output_variance: float32 [1, 2048, 2048], P(None, ('ctx', 'fsdp'))
- gate_grad: float32 [1, 5632, 2048], P(None, ('ctx', 'fsdp'))
- gate_update: float32 [1, 5632, 2048], P(None, ('ctx', 'fsdp'))
- gate_momentum: float32 [1, 5632, 2048], P(None, ('ctx', 'fsdp'))
- gate_variance: float32 [1, 5632, 2048], P(None, ('ctx', 'fsdp'))
- up_grad: float32 [1, 5632, 2048], P(None, ('ctx', 'fsdp'))
- up_update: float32 [1, 5632, 2048], P(None, ('ctx', 'fsdp'))
- up_momentum: float32 [1, 5632, 2048], P(None, ('ctx', 'fsdp'))
- up_variance: float32 [1, 5632, 2048], P(None, ('ctx', 'fsdp'))
- down_grad: float32 [1, 5632, 2048], P(None, ('ctx', 'fsdp'))
- down_update: float32 [1, 5632, 2048], P(None, ('ctx', 'fsdp'))
- down_momentum: float32 [1, 5632, 2048], P(None, ('ctx', 'fsdp'))
- down_variance: float32 [1, 5632, 2048], P(None, ('ctx', 'fsdp'))
- gains_grad: float32 [1, 2048, 2], P(None, ('ctx', 'fsdp'))
- gains_update: float32 [1, 2048, 2], P(None, ('ctx', 'fsdp'))
- gains_momentum: float32 [1, 2048, 2], P(None, ('ctx', 'fsdp'))
- gains_variance: float32 [1, 2048, 2], P(None, ('ctx', 'fsdp'))
The draws below stay inside these ranges and needn't reach their ends.
Inputs may be any that keep to these rules, and one draw needn't show every extreme that they name: `block_table`: in each row, stored blocks 2c and 2c + 1 hold logical blocks b and 2 * 8 - 1 - b; every row is a permutation. `positions`: strictly rising in logical order; the first logical token of each sequence has 0, the last 2047.
All inputs are finite; a program needn't handle non-finite values.
Results may differ from the reference program's by a relative error of at most 0.024.
Values may be sent and summed in bfloat16 or wider, within the bound.
No kernel may reach another device: no remote copies, remote signals or barrier semaphores. Data moves between devices by JAX's collectives and lax.ppermute only.
A program may use at most 768 MiB of HBM per device.

```python
import math
import jax
import jax.numpy as jnp
from jax import lax

D = 2048
HEADS = 32
KV_HEADS = 4
HEAD = 64
FF = 5632
LEN = 1024
LAYERS = 1
STEP = 10
KVW = 256
SEQS = 16
TOKENS = 16384
N_CTX = 8


def pair_table(key):
    seq_keys = jax.random.split(key, SEQS)

    def shuffled(one_key):
        return jax.random.permutation(one_key, N_CTX)
    arranged = jax.vmap(shuffled)(seq_keys).astype(jnp.int32)
    flips = jax.random.randint(jax.random.fold_in(key, 11), (SEQS, N_CTX), 0, 2).astype(jnp.int32)
    highest = 2 * N_CTX - 1
    leading = jnp.where(flips == 1, highest - arranged, arranged)
    return jnp.stack([leading, highest - leading], -1).reshape(SEQS, 2 * N_CTX).astype(jnp.int32)


def draw_block_table(key, part):
    shared = pair_table(key)
    return shared


def draw_positions(key, part):
    shared = pair_table(key)
    key = jax.random.fold_in(key, 5)
    inner = 2 * LEN - 2
    scores = jax.random.randint(key, (SEQS, inner), 0, 65536).astype(jnp.int32) * inner + jnp.arange(inner, dtype=jnp.int32)[None, :]
    picked = lax.top_k(scores, LEN - 2)[1].astype(jnp.int32)
    chosen = jnp.sort(picked, -1) + 1
    starts = jnp.zeros((SEQS, 1), jnp.int32)
    ordered = jnp.concatenate([starts, chosen, starts + 2 * LEN - 1], 1)
    block_rows = LEN // (2 * N_CTX)
    logical = (shared[:, :, None] * block_rows + jnp.arange(block_rows, dtype=jnp.int32)[None, None, :]).reshape(SEQS, LEN)
    return jnp.take_along_axis(ordered, logical, 1).astype(jnp.int32)


def block_levels(own_key, extent, pieces, low, top_value):
    loudness, own = 1.0, jax.random.fold_in(own_key, 6)
    for axis_at, blocks in pieces:
        draws = jnp.exp(jax.random.uniform(jax.random.fold_in(own, axis_at), (blocks,), jnp.float32, low / len(pieces), top_value / len(pieces)))
        loudness = loudness * jnp.repeat(draws, extent[axis_at] // blocks).reshape([-1 if axis == axis_at else 1 for axis in range(len(extent))])
    return loudness


def centred(stream_key, shape, deviation, most, cuts=(), kind=jnp.bfloat16):
    drawn = deviation * jax.random.normal(stream_key, shape, jnp.float32)
    if cuts:
        drawn = drawn * block_levels(stream_key, shape, cuts, -0.22, 0.18)
    return jnp.clip(drawn, -most, most).astype(kind)


def setup_inputs(seed: int = 0) -> dict:
    key_list = jax.random.split(jax.random.key(seed), 29)
    return {
        "hidden_in": centred(key_list[0], (SEQS, LEN, D), 1.0, 6.0, ((0, 16), (1, 8))),
        "cotangent": centred(key_list[1], (SEQS, LEN, D), 1.0, 6.0, ((0, 16), (1, 8))),
        "block_table": draw_block_table(jax.random.fold_in(key_list[28], 71), 0),
        "positions": draw_positions(jax.random.fold_in(key_list[28], 71), 0),
        "query_weight": centred(key_list[4], (LAYERS, D, D), D ** -0.5, 0.125, ((1, 128),), jnp.float32),
        "key_weight": centred(key_list[5], (LAYERS, D, KVW), D ** -0.5, 0.125, ((1, 128),), jnp.float32),
        "value_weight": centred(key_list[6], (LAYERS, D, KVW), D ** -0.5, 0.125, ((1, 128),), jnp.float32),
        "output_weight": centred(key_list[7], (LAYERS, D, D), (max(4 * D // LEN, 1)) ** -0.5, 2.0, ((1, 128),), jnp.float32),
        "gate_weight": centred(key_list[8], (LAYERS, FF, D), D ** -0.5, 0.125, ((1, 128),), jnp.float32),
        "up_weight": centred(key_list[9], (LAYERS, FF, D), D ** -0.5, 0.125, ((1, 128),), jnp.float32),
        "down_weight": centred(key_list[10], (LAYERS, FF, D), FF ** -0.5, 0.078125, ((1, 128),), jnp.float32),
        "norm_gains": jnp.clip(1.0 + 0.1 * jax.random.normal(key_list[11], (LAYERS, D, 2), jnp.float32), 0.5, 1.5),
        "query_first": centred(key_list[12], (LAYERS, D, D), (0.11 * TOKENS ** 0.5), 80.0, ((1, 128),), jnp.float32),
        "key_first": centred(key_list[13], (LAYERS, D, KVW), (0.33 * TOKENS ** 0.5), 256.0, ((1, 128),), jnp.float32),
        "value_first": centred(key_list[14], (LAYERS, D, KVW), (0.33 * TOKENS ** 0.5), 256.0, ((1, 128),), jnp.float32),
        "output_first": centred(key_list[15], (LAYERS, D, D), (0.22 * SEQS ** 0.5), 6.0, ((1, 128),), jnp.float32),
        "gate_first": centred(key_list[16], (LAYERS, FF, D), (0.039 * TOKENS ** 0.5), 32.0, ((1, 128),), jnp.float32),
        "up_first": centred(key_list[17], (LAYERS, FF, D), (0.039 * TOKENS ** 0.5), 32.0, ((1, 128),), jnp.float32),
        "down_first": centred(key_list[18], (LAYERS, FF, D), (0.066 * TOKENS ** 0.5), 48.0, ((1, 128),), jnp.float32),
        "gains_first": centred(key_list[19], (LAYERS, D, 2), (0.16 * TOKENS ** 0.5), 128.0, ((1, 128),), jnp.float32),
        "query_second": jnp.clip(jnp.exp(math.log(6881.28) - 2.7821581 * jax.random.uniform(key_list[20], (LAYERS, D, D), jnp.float32) ** block_levels(key_list[20], (LAYERS, D, D), ((1, 128),), -0.2, 0.2)), 425.984, 6881.28),
        "key_second": jnp.clip(jnp.exp(math.log(62259.2) - 2.7621174 * jax.random.uniform(key_list[21], (LAYERS, D, KVW), jnp.float32) ** block_levels(key_list[21], (LAYERS, D, KVW), ((1, 128),), -0.2, 0.2)), 3932.16, 62259.2),
        "value_second": jnp.clip(jnp.exp(math.log(62259.2) - 2.7621174 * jax.random.uniform(key_list[22], (LAYERS, D, KVW), jnp.float32) ** block_levels(key_list[22], (LAYERS, D, KVW), ((1, 128),), -0.2, 0.2)), 3932.16, 62259.2),
        "output_second": jnp.clip(jnp.exp(math.log(27.2) - 2.8332134 * jax.random.uniform(key_list[23], (LAYERS, D, D), jnp.float32) ** block_levels(key_list[23], (LAYERS, D, D), ((1, 128),), -0.2, 0.2)), 1.6, 27.2),
        "gate_second": jnp.clip(jnp.exp(math.log(835.584) - 2.7686748 * jax.random.uniform(key_list[24], (LAYERS, FF, D), jnp.float32) ** block_levels(key_list[24], (LAYERS, FF, D), ((1, 128),), -0.2, 0.2)), 52.4288, 835.584),
        "up_second": jnp.clip(jnp.exp(math.log(835.584) - 2.7686748 * jax.random.uniform(key_list[25], (LAYERS, FF, D), jnp.float32) ** block_levels(key_list[25], (LAYERS, FF, D), ((1, 128),), -0.2, 0.2)), 52.4288, 835.584),
        "down_second": jnp.clip(jnp.exp(math.log(2457.6) - 2.7699257 * jax.random.uniform(key_list[26], (LAYERS, FF, D), jnp.float32) ** block_levels(key_list[26], (LAYERS, FF, D), ((1, 128),), -0.2, 0.2)), 154.0096, 2457.6),
        "gains_second": jnp.clip(jnp.exp(math.log(15564.8) - 2.7789245 * jax.random.uniform(key_list[27], (LAYERS, D, 2), jnp.float32) ** block_levels(key_list[27], (LAYERS, D, 2), ((1, 128),), -0.2, 0.2)), 966.656, 15564.8),
    }


EPS = 1e-05
NEG = -1e+30
BETA_ONE = 0.9
BETA_TWO = 0.95
ADAM_EPS = 1e-08
RATES = (0.1, 0.1, 0.1, 1.5, 0.1, 0.1, 0.066, 0.5)
DECAYS = (0.1, 0.1, 0.1, 0.1, 0.1, 0.1, 0.1, 0.0)

@jax.custom_vjp
def low(v):
    return lax.optimization_barrier(v.astype(jnp.bfloat16)).astype(jnp.float32)

@jax.custom_vjp
def low_back(v):
    return v

def low_keep(v):
    return (low(v), None)

def low_pass(kept, grad):
    return (grad,)

def back_keep(v):
    return (v, None)

def back_low(kept, grad):
    return (low(grad),)
low.defvjp(low_keep, low_pass)
low_back.defvjp(back_keep, back_low)

def rope_tables(places):
    half = HEAD // 2
    freqs = jnp.exp(jnp.arange(half, dtype=jnp.float32) * (-2.0 * math.log(10000.0) / HEAD))
    angles = places.astype(jnp.float32)[:, None] * freqs[None, :]
    return (jnp.cos(angles)[:, None, :], jnp.sin(angles)[:, None, :])

def rotate(vector, cosine, sine):
    half = vector.shape[-1] // 2
    first_half = vector[..., :half]
    second_half = vector[..., half:]
    return jnp.concatenate([first_half * cosine - second_half * sine, second_half * cosine + first_half * sine], -1)

def product(left, right):
    return jnp.dot(left, right, precision=lax.Precision.HIGHEST, preferred_element_type=jnp.float32)

def rms_scale(values):
    return lax.rsqrt(lax.optimization_barrier(jnp.mean(values * values, -1, keepdims=True)) + EPS)

def layer_forward(state, params, order, cosine, sine):
    w_query, w_key, w_value, w_output, w_gate, w_up, w_down, gains = [low(p) for p in params]
    groups = HEADS // KV_HEADS
    length = state.shape[0]
    normed_one = low(state * rms_scale(state) * gains[:, 0])
    queries = low_back(product(normed_one, w_query)).reshape(length, HEADS, HEAD)
    keys = low_back(product(normed_one, w_key)).reshape(length, KV_HEADS, HEAD)
    values = low(low_back(product(normed_one, w_value))).reshape(length, KV_HEADS, HEAD)
    query_rot = low(rotate(queries, cosine, sine)).reshape(length, KV_HEADS, groups, HEAD)
    key_rot = low(rotate(keys, cosine, sine))
    rows = min(512, length)

    def attend(inputs):
        query_block, order_block = inputs
        raw = jnp.einsum('tkgd,nkd->kgtn', query_block, key_rot, precision=lax.Precision.HIGHEST)
        scores = low_back(raw) * HEAD ** (-0.5)
        scores = jnp.where(order[None, :] <= order_block[:, None], scores, NEG)
        peak = lax.optimization_barrier(jnp.max(scores, -1, keepdims=True))
        expo = jnp.exp(scores - peak)
        probs = low(expo / lax.optimization_barrier(jnp.sum(expo, -1, keepdims=True)))
        return jnp.einsum('kgtn,nkd->tkgd', probs, values, precision=lax.Precision.HIGHEST)
    mixed = lax.map(jax.checkpoint(attend), (query_rot.reshape(length // rows, rows, KV_HEADS, groups, HEAD), order.reshape(length // rows, rows)))
    mixed_low = low(low_back(mixed.reshape(length, D)))
    residual_one = state + low_back(product(mixed_low, w_output))
    normed_two = low(residual_one * rms_scale(residual_one) * gains[:, 1])
    gate = low_back(product(normed_two, w_gate.T))
    up_proj = low_back(product(normed_two, w_up.T))
    hidden = low(gate * jax.nn.sigmoid(gate) * up_proj)
    return residual_one + low_back(product(hidden, w_down))

def adam_step(weight, first, second, grad, rate, decay):
    momentum = BETA_ONE * first + (1.0 - BETA_ONE) * grad
    variance = BETA_TWO * second + (1.0 - BETA_TWO) * grad * grad
    corrected = momentum / (1.0 - BETA_ONE ** STEP)
    root = jnp.sqrt(variance / (1.0 - BETA_TWO ** STEP))
    update = weight - rate * (corrected / (root + ADAM_EPS) + decay * weight)
    return (update, momentum, variance)

def reference(hidden_in, cotangent, block_table, positions, query_weight, key_weight, value_weight, output_weight, gate_weight, up_weight, down_weight, norm_gains, query_first, key_first, value_first, output_first, gate_first, up_first, down_first, gains_first, query_second, key_second, value_second, output_second, gate_second, up_second, down_second, gains_second):
    weights = (query_weight, key_weight, value_weight, output_weight, gate_weight, up_weight, down_weight, norm_gains)
    firsts = (query_first, key_first, value_first, output_first, gate_first, up_first, down_first, gains_first)
    seconds = (query_second, key_second, value_second, output_second, gate_second, up_second, down_second, gains_second)
    block_rows = LEN // (2 * N_CTX)
    logical = (block_table[:, :, None] * block_rows + jnp.arange(block_rows, dtype=jnp.int32)[None, None, :]).reshape(SEQS, LEN).astype(jnp.int32)

    def forward(state_all, params):

        def one_sequence(carry, inputs):
            state, order, places = inputs
            cosine, sine = rope_tables(places)
            for layer_index in range(LAYERS):
                state = layer_forward(state, tuple((p[layer_index] for p in params)), order, cosine, sine)
            return (carry, state)
        _, outputs = lax.scan(one_sequence, jnp.zeros((), jnp.float32), (state_all, logical, positions))
        return outputs
    params = tuple((w.astype(jnp.float32) for w in weights))
    result, pullback = jax.vjp(forward, hidden_in.astype(jnp.float32), params)
    hidden_grad, grads = pullback(cotangent.astype(jnp.float32))
    fresh = [adam_step(weights[i], firsts[i], seconds[i], grads[i], RATES[i], DECAYS[i]) for i in range(8)]
    return (result.astype(jnp.bfloat16), hidden_grad, grads[0], fresh[0][0], fresh[0][1], fresh[0][2], grads[1], fresh[1][0], fresh[1][1], fresh[1][2], grads[2], fresh[2][0], fresh[2][1], fresh[2][2], grads[3], fresh[3][0], fresh[3][1], fresh[3][2], grads[4], fresh[4][0], fresh[4][1], fresh[4][2], grads[5], fresh[5][0], fresh[5][1], fresh[5][2], grads[6], fresh[6][0], fresh[6][1], fresh[6][2], grads[7], fresh[7][0], fresh[7][1], fresh[7][2])
```

```python
import functools
import math

import jax
import jax.numpy as jnp
from jax import lax
from jax.experimental import pallas as pl
from jax.experimental.pallas import tpu as pltpu
from jax.sharding import PartitionSpec as P

D = 2048
HEADS = 32
KV_HEADS = 4
HEAD = 64
FF = 5632
STEP = 10
N_CTX = 8
N_X = 4
MINE = HEADS // N_X
WIDE = MINE * HEAD
PACK = WIDE + 2 * HEAD
UNITS = 44
PADDED = 48

EPS = 1e-05
NEG = -1e30
BETA_ONE = 0.9
BETA_TWO = 0.95
ADAM_EPS = 1e-08
RATES = (0.1, 0.1, 0.1, 1.5, 0.1, 0.1, 0.066, 0.5)
DECAYS = (0.1, 0.1, 0.1, 0.1, 0.1, 0.1, 0.1, 0.0)
BY_COLUMN = (((1,), (1,)), ((), ()))
BY_ROW = (((0,), (0,)), ((), ()))
bf16 = jnp.bfloat16
f32 = jnp.float32

AXES = ("x", "zl", "zh", "y", "core")
SHARE = ("zh", "zl", "y")
SWAP = [(0, 1), (1, 0)]
RING_X = ("x", [(i, (i + 1) % 4) for i in range(4)], [(i, (i - 1) % 4) for i in range(4)])
RING_Y = ("y",) + RING_X[1:]
DEPTH = (0, 2, 1, 3)
RING_Z = (
    ("zl", "zh"),
    [(DEPTH[i], DEPTH[(i + 1) % 4]) for i in range(4)],
    [(DEPTH[i], DEPTH[(i - 1) % 4]) for i in range(4)],
)
STEPS = (0, -1, 1, 2)


def across(ring):
    there = dict(ring[1])
    return [(i, there[there[i]]) for i in there]


def after(value, *others):
    return lax.optimization_barrier((value,) + others)[0]


def add(*terms):
    total = terms[0].astype(f32)
    for term in terms[1:]:
        total = total + term.astype(f32)
    return total


def place(blocks, spots, axis):
    shape = list(blocks[0].shape)
    shape.insert(axis, len(blocks))
    whole = jnp.zeros(shape, blocks[0].dtype)
    for block, spot in zip(blocks, spots):
        at = [0] * len(shape)
        at[axis] = spot
        whole = lax.dynamic_update_slice(whole, jnp.expand_dims(block, axis), tuple(at))
    return whole


def ring_halves(block, ring):
    name, right, left = ring
    half = block.shape[0] // 2
    from_left = lax.ppermute(block, name, right)
    from_right = lax.ppermute(block, name, left)
    first = lax.ppermute(from_left[:half], name, right)
    second = lax.ppermute(from_right[half:], name, left)
    return [block, from_left, from_right, first, second]


def ring_small(block, ring):
    name, right, left = ring
    return [
        block,
        lax.ppermute(block, name, right),
        lax.ppermute(block, name, left),
        lax.ppermute(block, name, across(ring)),
    ]


def ring_sum_small(own, to_left, to_right, far, ring):
    name, right, left = ring
    return add(
        own,
        lax.ppermute(to_left, name, left),
        lax.ppermute(to_right, name, right),
        lax.ppermute(far, name, across(ring)),
    )


def gather_x_core(block):
    blocks = ring_halves(block, RING_X)
    return blocks + [lax.ppermute(b, "core", SWAP) for b in blocks]


def ring_spots():
    at = lax.axis_index("x"), lax.axis_index("y")
    side, far_side, core = (lax.axis_index(n) for n in ("zl", "zh", "core"))
    spots_x, spots_y = ([(a + step) % 4 for step in STEPS] for a in at)
    depth = [(far_side * 2 + side + step) % 4 for step in STEPS]
    spots_z = [d % 2 * 2 + d // 2 for d in depth]
    return spots_x, spots_y, spots_z, [core, 1 - core]


def pick(value, spot, axis):
    return lax.dynamic_index_in_dim(value, spot, axis, False)


def rope_tables(places):
    half = HEAD // 2
    freqs = jnp.exp(jnp.arange(half, dtype=f32) * (-2.0 * math.log(10000.0) / HEAD))
    angles = places.astype(f32)[:, None] * freqs[None, :]
    return jnp.cos(angles), jnp.sin(angles)


def dot(left, right, dims, kind):
    return lax.dot_general(left, right, dims, preferred_element_type=f32).astype(kind)


def adam_step(weight, first, second, grad, rate, decay):
    momentum = BETA_ONE * first + (1.0 - BETA_ONE) * grad
    variance = BETA_TWO * second + (1.0 - BETA_TWO) * grad * grad
    corrected = momentum / (1.0 - BETA_ONE**STEP)
    root = jnp.sqrt(variance / (1.0 - BETA_TWO**STEP))
    update = weight - rate * (corrected / (root + ADAM_EPS) + decay * weight)
    return (update, momentum, variance)


def call(kernel, outs, ins, scratch=(), prefetch=(), flops=0, traffic=0):
    spec_any = pl.BlockSpec(memory_space=pl.ANY)
    spec_vmem = pl.BlockSpec(memory_space=pltpu.VMEM)
    spec_smem = pl.BlockSpec(memory_space=pltpu.SMEM)
    return pl.pallas_call(
        kernel,
        out_shape=[jax.ShapeDtypeStruct(shape, kind) for shape, kind in outs],
        in_specs=[spec_smem] * len(prefetch)
        + [spec_vmem if inside else spec_any for _, inside in ins],
        out_specs=[spec_vmem] * len(outs),
        scratch_shapes=list(scratch),
        compiler_params=pltpu.CompilerParams(vmem_limit_bytes=56 * 1024 * 1024),
        cost_estimate=pl.CostEstimate(flops=flops, bytes_accessed=traffic, transcendentals=0),
    )(*prefetch, *(array for array, _ in ins))


def matmul(left, right, dims=(((1,), (0,)), ((), ()))):
    return lax.dot_general(left, right, dims, preferred_element_type=f32)


def lanes(shape):
    return lax.broadcasted_iota(jnp.int32, shape, 1)


def prepare_kernel(state_ref, table_ref, out_ref):
    value = state_ref[...].astype(f32)
    scale = lax.rsqrt(jnp.mean(value * value, -1, keepdims=True) + EPS)
    out_ref[:, :D] = (value * scale).astype(bf16)
    out_ref[:, D:] = table_ref[...]


def join_kernel(*refs):
    at = 0
    for ref in refs[:-1]:
        refs[-1][at : at + ref.shape[0], :] = ref[...]
        at += ref.shape[0]


def join(blocks):
    shape = (sum(b.shape[0] for b in blocks), blocks[0].shape[1])
    return call(join_kernel, [(shape, blocks[0].dtype)], [(b, True) for b in blocks])[0]


def output_kernel(res_ref, own, left, right, low, high, out_ref):
    for at, part in zip((0, 64), sum_arrived(own, left, right, low, high)):
        rows = slice(at, at + 64)
        out_ref[rows, :] = (res_ref[rows, :] + part).astype(bf16)


def swap_halves(value):
    low = lanes(value.shape) % HEAD < HEAD // 2
    return jnp.where(low, pltpu.roll(value, 96, 1), pltpu.roll(value, 32, 1))


def rope_factors(angles):
    low = lanes(angles.shape) % HEAD < HEAD // 2
    cosine = jnp.where(low, angles, pltpu.roll(angles, 32, 1))
    sine = jnp.where(low, -pltpu.roll(angles, 96, 1), angles)
    return cosine, sine


PIECES = (128, 128, 128, 64, 64)


def starts(sizes):
    at, found = 0, []
    for size in sizes:
        found.append(at)
        at += size
    return found


def project_kernel(spots, *refs):
    tokens, weights = refs[:5], refs[5:13]
    query_ref, pair_ref, normed_ref, full_ref, gain_ref, angle_ref = refs[13:19]
    table_buf, weight_buf, sems = refs[19:]
    copies = []
    for i, (at, size) in enumerate(zip(starts(PIECES), PIECES)):
        rows = pl.ds(at, size)
        copies.append(
            pltpu.make_async_copy(tokens[i].at[:, pl.ds(0, D)], normed_ref.at[rows], sems.at[2 * i])
        )
        copies.append(
            pltpu.make_async_copy(
                tokens[i].at[:, pl.ds(D, 128)], table_buf.at[rows], sems.at[2 * i + 1]
            )
        )
    for i in range(8):
        copies.append(
            pltpu.make_async_copy(
                weights[i], weight_buf.at[i // 4, pl.ds(i % 4 * 256, 256)], sems.at[10 + i]
            )
        )
    for copy in copies:
        copy.start()
    for copy in copies:
        copy.wait()
    for side in range(2):
        for deep in range(4):
            for up in range(4):
                for along in range(4):
                    at = deep * 256 + up * 64 + along * 16
                    block = weight_buf[side, at : at + 16, :]
                    to = spots[along] * 4 + spots[8 + deep]
                    to = ((to * 4 + spots[4 + up]) * 2 + spots[12 + side]) * 16
                    to = pl.multiple_of(to, 16)
                    full_ref[pl.ds(to, 16), :] = block[:, :PACK]
                    gain_ref[pl.ds(to, 16), :] = block[:, PACK:]
    table = table_buf[...].astype(f32)
    angles = table + pltpu.roll(table, 64, 1)
    angle_ref[...] = angles
    for at in range(0, 512, 256):
        rows = slice(at, at + 256)
        cosine, sine = rope_factors(angles[rows])
        for col in range(0, PACK, 128):
            part = matmul(normed_ref[rows, :], full_ref[:, col : col + 128])
            turned = part * cosine + swap_halves(part) * sine
            if col < WIDE:
                query_ref[rows, col : col + 128] = (turned * HEAD**-0.5).astype(bf16)
            else:
                turned = jnp.where(lanes(part.shape) < HEAD, turned, part)
                pair_ref[rows, :] = turned.astype(bf16)


def attend_kernel(spots, *refs):
    query_ref, own_ref, other_ref, row_ref, column_ref = refs[:5]
    weights = refs[5:13]
    mixed_ref, sum_ref, full_ref, own_out, left_out, right_out, low_out, high_out = refs[13:21]
    weight_buf, key_buf, value_buf, sems = refs[21:]
    copies = []
    for i in range(8):
        copies.append(
            pltpu.make_async_copy(
                weights[i], weight_buf.at[i // 4, pl.ds(i % 4 * 64, 64)], sems.at[i]
            )
        )
    for copy in copies:
        copy.start()
    split_pairs(own_ref, other_ref, key_buf, value_buf)
    visible = column_ref[...] <= row_ref[...]
    logs = jnp.zeros((512, 128), f32)
    for pair in range(MINE // 2):
        cols = slice(pair * 128, pair * 128 + 128)
        both = query_ref[:, cols]
        mixed = jnp.zeros((512, 128), f32)
        for side in range(2):
            scores = matmul(both, key_buf[side], BY_COLUMN)
            scores = jnp.where(visible, scores, NEG)
            peak = jnp.max(scores, -1, keepdims=True)
            expo = jnp.exp(scores - peak)
            total = jnp.sum(expo, -1, keepdims=True)
            probs = (expo * (1.0 / total)).astype(bf16)
            mixed = mixed + matmul(probs, value_buf[side])
            logs = jnp.where(
                lanes(logs.shape) == pair * 2 + side, peak + jnp.log(total), logs
            )
        mixed_ref[:, cols] = mixed.astype(bf16)
    sum_ref[...] = logs
    for copy in copies:
        copy.wait()
    for side in range(2):
        for deep in range(4):
            for up in range(4):
                at = deep * 64 + up * 16
                to = (spots[8 + deep] * 4 + spots[4 + up]) * 2 + spots[12 + side]
                to = pl.multiple_of(to * 16, 16)
                full_ref[pl.ds(to, 16), :] = weight_buf[side, at : at + 16, :]
    put_parts(
        lambda at, size: matmul(mixed_ref[at : at + size, :], full_ref[...]).astype(bf16),
        (own_out, left_out, right_out, low_out, high_out),
    )


def split_pairs(own_ref, other_ref, key_buf, value_buf):
    for i, ref in enumerate((own_ref, other_ref)):
        rows = slice(i * 512, i * 512 + 512)
        pair = ref[...].astype(f32)
        low = lanes(pair.shape) < HEAD
        key, value = jnp.where(low, pair, 0.0), jnp.where(low, 0.0, pair)
        key_buf[0, rows, :] = key.astype(bf16)
        key_buf[1, rows, :] = pltpu.roll(key, HEAD, 1).astype(bf16)
        value_buf[0, rows, :] = pltpu.roll(value, HEAD, 1).astype(bf16)
        value_buf[1, rows, :] = value.astype(bf16)


def put_parts(rows_at, outs):
    own, left, right, low, high = outs
    value = rows_at(0, 256)
    own[...] = value[:128]
    low[...] = value[128:192]
    left[64:, :] = value[192:]
    value = rows_at(256, 256)
    right[64:, :] = value[:64]
    high[...] = value[64:128]
    left[:64, :] = value[128:192]
    right[:64, :] = value[192:]


def put_both(rows_at, outs):
    first, second = outs[5:]
    put_parts(rows_at, outs[:5])
    put_parts(
        lambda at, size: rows_at(512 + at, size),
        (
            second.at[pl.ds(0, 128)],
            first.at[pl.ds(0, 128)],
            first.at[pl.ds(128, 128)],
            second.at[pl.ds(128, 64)],
            second.at[pl.ds(192, 64)],
        ),
    )


PARTS = (((128, D), bf16), ((128, D), bf16), ((128, D), bf16), ((64, D), bf16), ((64, D), bf16))


def scatter_parts(parts):
    own, left, right, low, high = parts
    name, to_right, to_left = RING_X
    got_left = lax.ppermute(left, name, to_left)
    got_right = lax.ppermute(right, name, to_right)
    low = add(low, got_left[:64]).astype(bf16)
    high = add(high, got_right[:64]).astype(bf16)
    return own, got_left, got_right, lax.ppermute(low, name, to_left), lax.ppermute(high, name, to_right)


BOTH_PARTS = PARTS + (((256, D), bf16), ((256, D), bf16))


def scatter_both(parts):
    own, left, right, low, high, first, second = parts
    first = lax.ppermute(first, "core", SWAP)
    second = lax.ppermute(second, "core", SWAP)
    left = add(left, first[:128]).astype(bf16)
    right = add(right, first[128:]).astype(bf16)
    own = add(own, second[:128]).astype(bf16)
    low = add(low, second[128:192]).astype(bf16)
    high = add(high, second[192:]).astype(bf16)
    return scatter_parts((own, left, right, low, high))


def sum_arrived(own, got_left, got_right, low, high):
    first = own[:64, :].astype(f32) + got_right[64:, :].astype(f32) + low[...].astype(f32)
    second = own[64:, :].astype(f32) + got_left[64:, :].astype(f32) + high[...].astype(f32)
    return first, second


def residual_kernel(state_ref, gain_ref, own, left, right, low, high, out_ref, rows_ref):
    for at, part in zip((0, 64), sum_arrived(own, left, right, low, high)):
        rows = slice(at, at + 64)
        value = state_ref[rows, :].astype(f32) + part
        out_ref[rows, :] = value
        scale = lax.rsqrt(jnp.mean(value * value, -1, keepdims=True) + EPS)
        rows_ref[rows, :] = (value * scale * gain_ref[...]).astype(bf16)


def back_two_kernel(grad_ref, gain_ref, res_ref, own, left, right, low, high, out_ref, low_ref, term_ref):
    terms = jnp.zeros((1, D), f32)
    for at, part in zip((0, 64), sum_arrived(own, left, right, low, high)):
        rows = slice(at, at + 64)
        value = res_ref[rows, :]
        scale = lax.rsqrt(jnp.mean(value * value, -1, keepdims=True) + EPS)
        normed = value * scale
        terms = terms + jnp.sum(part * normed, 0, keepdims=True)
        weighted = part * gain_ref[...]
        through = scale * (weighted - normed * jnp.mean(weighted * normed, -1, keepdims=True))
        total = grad_ref[rows, :].astype(f32) + through
        out_ref[rows, :] = total
        low_ref[rows, :] = total.astype(bf16)
    term_ref[...] = terms


def back_one_kernel(grad_ref, state_ref, own, left, right, low, high, out_ref):
    for at, part in zip((0, 64), sum_arrived(own, left, right, low, high)):
        rows = slice(at, at + 64)
        value = state_ref[rows, :].astype(f32)
        scale = lax.rsqrt(jnp.mean(value * value, -1, keepdims=True) + EPS)
        normed = value * scale
        through = scale * (part - normed * jnp.mean(part * normed, -1, keepdims=True))
        out_ref[rows, :] = grad_ref[rows, :] + through


def mlp_kernel(*refs):
    tokens, grads, weight_ref = refs[:10], refs[10:20], refs[20]
    outs = refs[21:28]
    hidden_ref, dgate_ref, dup_ref, rows_ref, grads_ref = refs[28:33]
    weight_buf, sum_buf, sems = refs[33:]
    copies = []
    for kind in range(3):
        copies.append(
            pltpu.make_async_copy(
                weight_ref.at[:, pl.ds(kind * PADDED, PADDED)], weight_buf.at[kind], sems.at[kind]
            )
        )
    for i in range(10):
        at = starts(PIECES + PIECES)[i]
        rows = pl.ds(at, tokens[i].shape[0])
        copies.append(pltpu.make_async_copy(tokens[i], rows_ref.at[rows], sems.at[3 + i]))
        copies.append(pltpu.make_async_copy(grads[i], grads_ref.at[rows], sems.at[13 + i]))
    for copy in copies:
        copy.start()
    for copy in copies:
        copy.wait()

    def step(i, carry):
        rows = pl.ds(pl.multiple_of(i * 256, 256), 256)
        for col in range(0, 768, 384):
            cols = slice(col, col + 384)
            gate_w, up_w, down_w = (
                weight_buf[k, col // PADDED : (col + 384) // PADDED].reshape(384, D)
                for k in range(3)
            )
            gate = matmul(rows_ref[rows, :], gate_w, BY_COLUMN)
            up_proj = matmul(rows_ref[rows, :], up_w, BY_COLUMN)
            dhidden = matmul(grads_ref[rows, :], down_w, BY_COLUMN)
            sigmoid = 1.0 / (1.0 + jnp.exp(-gate))
            silu_gate = gate * sigmoid
            hidden_ref[rows, cols] = (silu_gate * up_proj).astype(bf16)
            slope = sigmoid * (1.0 + gate * (1.0 - sigmoid))
            dgate_ref[rows, cols] = (dhidden * up_proj * slope).astype(bf16)
            dup_ref[rows, cols] = (dhidden * silu_gate).astype(bf16)
        summed = matmul(dgate_ref[rows, :], weight_buf[0].reshape(768, D))
        summed = summed + matmul(dup_ref[rows, :], weight_buf[1].reshape(768, D))
        sum_buf[rows, :] = summed.astype(bf16)
        return carry

    lax.fori_loop(0, 4, step, 0)
    put_both(lambda at, size: sum_buf[at : at + size, :], outs)


def mlp_grad_kernel(left_ref, right_ref, *refs):
    out_ref = refs[-1]
    terms = matmul(left_ref[...], right_ref[...], BY_ROW).astype(bf16)
    out_ref[...] = terms.reshape(16, PADDED, terms.shape[1])


def mlp_grad(kind, left, right, before):
    width = 512
    held = [] if before is None else [before]
    return pl.pallas_call(
        mlp_grad_kernel,
        grid=(D // width,),
        out_shape=jax.ShapeDtypeStruct((16, 3 * PADDED, D), bf16),
        in_specs=[
            pl.BlockSpec((1024, 768), lambda i: (0, 0)),
            pl.BlockSpec((1024, width), lambda i: (0, i)),
        ]
        + [pl.BlockSpec(memory_space=pl.ANY)] * len(held),
        out_specs=pl.BlockSpec((16, PADDED, width), lambda i, kind=kind: (0, kind, i)),
        input_output_aliases={2: 0} if held else {},
        compiler_params=pltpu.CompilerParams(vmem_limit_bytes=40 * 1024 * 1024),
        cost_estimate=pl.CostEstimate(
            flops=2 * 1024 * 768 * D, bytes_accessed=8 * 2**20, transcendentals=0
        ),
    )(left, right, *held)


def branch_kernel(hidden_ref, weight_ref, *refs):
    outs, weight_buf, sem = refs[:7], refs[7], refs[8]
    copy = pltpu.make_async_copy(
        weight_ref.at[:, pl.ds(2 * PADDED, PADDED)], weight_buf, sem.at[0]
    )
    copy.start()
    copy.wait()
    put_both(
        lambda at, size: matmul(
            hidden_ref[at : at + size, :], weight_buf[...].reshape(768, D)
        ).astype(bf16),
        outs,
    )


def unmix_kernel(*refs):
    pieces, full_ref = refs[:5], refs[5]
    joined_ref, dmixed_ref, sems = refs[6:]
    copies = []
    for i, (at, size) in enumerate(zip(starts(PIECES), PIECES)):
        copies.append(pltpu.make_async_copy(pieces[i], joined_ref.at[pl.ds(at, size)], sems.at[i]))
    for copy in copies:
        copy.start()
    for copy in copies:
        copy.wait()
    for at in range(0, 512, 256):
        dmixed_ref[at : at + 256, :] = matmul(
            joined_ref[at : at + 256, :], full_ref[...], BY_COLUMN
        ).astype(bf16)


def attend_back_kernel(pair, query_ref, own_ref, other_ref, row_ref, column_ref, sum_ref, mixed_ref,
                       dmixed_ref, angle_ref, *refs):
    before = refs[0] if pair else None
    dquery_ref, dpair_ref, key_buf, value_buf = refs[1 if pair else 0 :]
    split_pairs(own_ref, other_ref, key_buf, value_buf)
    visible = column_ref[...] <= row_ref[...]
    cols = slice(pair * 128, pair * 128 + 128)
    both, dboth = query_ref[:, cols], dmixed_ref[:, cols]
    product = dboth.astype(f32) * mixed_ref[:, cols].astype(f32)
    low = lanes(product.shape) < HEAD
    dquery = jnp.zeros((512, 128), f32)
    dkeys, dvalues = [], []
    for side in range(2):
        delta = jnp.sum(jnp.where(low == (side == 0), product, 0.0), -1, keepdims=True)
        head = pair * 2 + side
        logs = sum_ref[:, head : head + 1]
        scores = matmul(both, key_buf[side], BY_COLUMN)
        probs = jnp.exp(jnp.where(visible, scores, NEG) - logs)
        dprobs = matmul(dboth, value_buf[side], BY_COLUMN)
        dscores = (probs * (dprobs - delta)).astype(bf16)
        dquery = dquery + matmul(dscores, key_buf[side])
        dkeys.append(matmul(dscores, both, BY_ROW))
        dvalues.append(matmul(probs.astype(bf16), dboth, BY_ROW))
    cosine, sine = rope_factors(angle_ref[...])
    dquery = dquery * HEAD**-0.5
    dquery_ref[...] = (dquery * cosine - swap_halves(dquery) * sine).astype(bf16)
    low = lanes((1024, 128)) < HEAD
    dkey = dkeys[0] + pltpu.roll(dkeys[1], HEAD, 1)
    dvalue = pltpu.roll(dvalues[0], HEAD, 1) + dvalues[1]
    total = jnp.where(low, dkey, dvalue)
    if pair:
        total = total + before[...]
    dpair_ref[...] = total


def finish_kernel(query0, query1, query2, query3, dpair_ref, got_ref, angle_ref, full_ref,
                  proj_ref, own_out, left_out, right_out, low_out, high_out):
    for i, ref in enumerate((query0, query1, query2, query3)):
        proj_ref[:, i * 128 : i * 128 + 128] = ref[...]
    total = dpair_ref[:512, :] + got_ref[...].astype(f32)
    cosine, sine = rope_factors(angle_ref[...])
    turned = total * cosine - swap_halves(total) * sine
    total = jnp.where(lanes(total.shape) < HEAD, turned, total)
    proj_ref[:, WIDE:] = total.astype(bf16)
    put_parts(
        lambda at, size: matmul(proj_ref[at : at + size, :], full_ref[...], BY_COLUMN).astype(bf16),
        (own_out, left_out, right_out, low_out, high_out),
    )


def terms_kernel(normed_ref, proj_ref, gain_ref, out_ref):
    for at in range(0, D, 512):
        rows = slice(at, at + 512)
        out_ref[rows, :PACK] = matmul(normed_ref[:, rows], proj_ref[...], BY_ROW).astype(bf16)
    out_ref[:, PACK:] = gain_ref[...]


def body(
    hidden_in,
    cotangent,
    block_table,
    positions,
    query_weight,
    key_weight,
    value_weight,
    output_weight,
    gate_weight,
    up_weight,
    down_weight,
    norm_gains,
    *moments,
):
    weights = (
        query_weight,
        key_weight,
        value_weight,
        output_weight,
        gate_weight,
        up_weight,
        down_weight,
        norm_gains,
    )
    firsts, seconds = moments[:8], moments[8:]
    tokens = hidden_in.shape[1]
    block_rows = tokens // 2
    spots_x, spots_y, spots_z, spots_core = ring_spots()
    at_side = lax.axis_index("zl")
    places = [spot * 2 + (at_side ^ flip) for flip in range(2) for spot in spots_x]
    table = block_table[0].reshape(N_CTX, 2)[jnp.stack(places)].reshape(-1)
    logical = (
        table[:, None] * block_rows + jnp.arange(block_rows, dtype=jnp.int32)[None, :]
    ).reshape(-1)

    mlp_rows = jnp.concatenate(
        [
            jnp.pad(w[0].astype(bf16), ((0, PADDED - UNITS), (0, 0)))
            for w in (gate_weight, up_weight, down_weight)
        ],
        0,
    )
    mlp_full = lax.all_gather(mlp_rows, SHARE, axis=0, tiled=True)
    mlp_full = mlp_full.reshape(-1, 3 * PADDED, D)

    gains = norm_gains[0].astype(bf16).astype(f32)
    gain_one = gains[:, :1]
    low = [w[0].astype(bf16).astype(f32) for w in (query_weight, key_weight, value_weight)]
    scaled = [(w * gain_one).astype(bf16) for w in low]
    rows = scaled[0].shape[0]
    packed = jnp.concatenate(
        [w.reshape(rows, N_X, -1).transpose(1, 0, 2) for w in scaled]
        + [jnp.broadcast_to(gains[:, 1:].astype(bf16), (N_X, rows, 128))],
        -1,
    )
    name, right, left = RING_X
    owned = join(
        [
            pick(packed, spots_x[0], 0),
            lax.ppermute(pick(packed, spots_x[2], 0), name, right),
            lax.ppermute(pick(packed, spots_x[1], 0), name, left),
            lax.ppermute(pick(packed, spots_x[3], 0), name, across(RING_X)),
        ]
    )
    owned = ring_small(join(ring_small(owned, RING_Y)), RING_Z)
    weight_pieces = owned + [lax.ppermute(b, "core", SWAP) for b in owned]

    state = hidden_in[0]
    tables = jnp.concatenate(rope_tables(positions[0]), 1)
    tables_low = tables.astype(bf16)
    rest = (tables - tables_low.astype(f32)).astype(bf16)
    sent = call(
        prepare_kernel,
        [((tokens, D + 128), bf16)],
        [(state, True), (jnp.concatenate([tables_low, rest], 1), True)],
    )[0]
    token_pieces = ring_halves(sent, RING_X)
    spots = jnp.stack(spots_x + spots_y + spots_z + spots_core).astype(jnp.int32)
    query, own_pair, normed_all, qkv_full, gain_rows, angles = call(
        project_kernel,
        [
            ((512, WIDE), bf16),
            ((512, 128), bf16),
            ((512, D), bf16),
            ((D, PACK), bf16),
            ((D, 128), bf16),
            ((512, 128), f32),
        ],
        [(v, False) for v in token_pieces + weight_pieces],
        scratch=[
            pltpu.VMEM((512, 128), bf16),
            pltpu.VMEM((2, 1024, PACK + 128), bf16),
            pltpu.SemaphoreType.DMA((18,)),
        ],
        prefetch=[spots],
        flops=2 * 512 * D * PACK,
        traffic=12 * 2**20,
    )
    gain_two = gain_rows[:, 0].astype(f32)[None]

    output_low = after(output_weight[0].astype(bf16), owned[3])
    output_low = ring_small(join(ring_small(output_low, RING_Y)), RING_Z)
    output_pieces = output_low + [lax.ppermute(b, "core", SWAP) for b in output_low]
    grad_pieces = gather_x_core(after(cotangent[0], query))

    other_pair = lax.ppermute(own_pair, "zl", SWAP)
    row, column = logical[:512, None], logical[None, :]
    mixed, logs, output_full, *parts = call(
        attend_kernel,
        [((512, WIDE), bf16), ((512, 128), f32), ((WIDE, D), bf16)] + list(PARTS),
        [(v, True) for v in (query, own_pair, other_pair, row, column)]
        + [(v, False) for v in output_pieces],
        scratch=[
            pltpu.VMEM((2, 256, D), bf16),
            pltpu.VMEM((2, 1024, 128), bf16),
            pltpu.VMEM((2, 1024, 128), bf16),
            pltpu.SemaphoreType.DMA((8,)),
        ],
        prefetch=[spots],
        flops=2 * 512 * D * WIDE + 4 * 8 * 512 * 1024 * 256,
        traffic=12 * 2**20,
    )
    residual, mlp_in = call(
        residual_kernel,
        [((tokens, D), f32), ((tokens, D), bf16)],
        [(v, True) for v in (state, gain_two) + scatter_parts(parts)],
    )

    row_pieces = gather_x_core(mlp_in)
    *parts, hidden, dgate, dup, rows_in, grad_rows = call(
        mlp_kernel,
        list(BOTH_PARTS) + [((1024, 768), bf16)] * 3 + [((1024, D), bf16)] * 2,
        [(v, False) for v in row_pieces + grad_pieces + [mlp_full]],
        scratch=[
            pltpu.VMEM((3, 16, PADDED, D), bf16),
            pltpu.VMEM((1024, D), bf16),
            pltpu.SemaphoreType.DMA((23,)),
        ],
        flops=10 * 1024 * 768 * D,
        traffic=30 * 2**20,
    )
    arrived = scatter_both(parts)
    terms = None
    for kind, (over, under) in enumerate(
        ((dgate, rows_in), (dup, rows_in), (hidden, grad_rows))
    ):
        terms = mlp_grad(kind, over, under, terms)
    mlp_terms = lax.psum_scatter(
        terms.reshape(-1, D), SHARE, scatter_dimension=0, tiled=True
    )
    mlp_grads = mlp_terms.astype(f32).reshape(3, PADDED, D)[:, :UNITS]

    grad_one, grad_low, gain_terms = call(
        back_two_kernel,
        [((tokens, D), f32), ((tokens, D), bf16), ((1, D), f32)],
        [(v, True) for v in (cotangent[0], gain_two, residual) + arrived],
    )
    grad_one_pieces = ring_halves(grad_low, RING_X)
    gain_terms = jnp.broadcast_to(gain_terms.reshape(D, 1), (D, 128)).astype(bf16)

    attn_grad, dmixed = call(
        unmix_kernel,
        [((512, D), bf16), ((512, WIDE), bf16)],
        [(v, False) for v in grad_one_pieces] + [(output_full, True)],
        scratch=[pltpu.SemaphoreType.DMA((5,))],
        flops=2 * 512 * D * WIDE,
        traffic=6 * 2**20,
    )
    output_terms = dot(mixed, attn_grad, BY_ROW, bf16).reshape(4, 4, 2, rows, D)
    given = lax.ppermute(pick(output_terms, spots_core[1], 2), "core", SWAP)
    output_terms = add(pick(output_terms, spots_core[0], 2), given).astype(bf16)
    output_terms = ring_sum_small(*(pick(output_terms, spot, 0) for spot in spots_z), RING_Z)
    output_terms = output_terms.astype(bf16)
    output_grad = ring_sum_small(*(pick(output_terms, spot, 0) for spot in spots_y), RING_Y)
    dqueries, dpair = [], None
    for pair in range(MINE // 2):
        dquery, dpair = call(
            functools.partial(attend_back_kernel, pair),
            [((512, 128), bf16), ((1024, 128), f32)],
            [
                (v, True)
                for v in (query, own_pair, other_pair, row, column, logs, mixed, dmixed, angles)
            ]
            + ([(dpair, True)] if pair else []),
            scratch=[pltpu.VMEM((2, 1024, 128), bf16)] * 2,
            flops=10 * 2 * 512 * 1024 * 256,
            traffic=4 * 2**20,
        )
        dqueries.append(dquery)
    got = lax.ppermute(dpair[512:].astype(bf16), "zl", SWAP)
    dprojected, *parts = call(
        finish_kernel,
        [((512, PACK), bf16)] + list(PARTS),
        [(v, True) for v in dqueries + [dpair, got, angles, qkv_full]],
        flops=2 * 512 * D * PACK,
        traffic=8 * 2**20,
    )
    hidden_grad = call(
        back_one_kernel,
        [((tokens, D), f32)],
        [(v, True) for v in (grad_one, state) + scatter_parts(parts)],
    )[0]
    branch = call(
        branch_kernel,
        BOTH_PARTS,
        [(after(hidden, dmixed), True), (mlp_full, False)],
        scratch=[pltpu.VMEM((16, PADDED, D), bf16), pltpu.SemaphoreType.DMA((1,))],
        flops=2 * 1024 * 768 * D,
        traffic=8 * 2**20,
    )
    hidden_out = call(
        output_kernel,
        [((tokens, D), bf16)],
        [(v, True) for v in (residual,) + scatter_both(branch)],
    )[0]

    qkv_terms = call(
        terms_kernel,
        [((D, PACK + 128), bf16)],
        [(v, True) for v in (normed_all, dprojected, gain_terms)],
        flops=2 * 512 * D * PACK,
        traffic=6 * 2**20,
    )[0]
    qkv_terms = qkv_terms.reshape(N_X, 4, 4, 2, rows, -1)
    given = lax.ppermute(pick(qkv_terms, spots_core[1], 3), "core", SWAP)
    qkv_terms = add(pick(qkv_terms, spots_core[0], 3), given).astype(bf16)
    qkv_terms = ring_sum_small(*(pick(qkv_terms, spot, 1) for spot in spots_z), RING_Z)
    qkv_terms = qkv_terms.astype(bf16)
    qkv_terms = ring_sum_small(*(pick(qkv_terms, spot, 1) for spot in spots_y), RING_Y)
    qkv_terms = qkv_terms.astype(bf16)
    qkv_grad = place(
        [
            pick(qkv_terms, spots_x[0], 0),
            lax.ppermute(pick(qkv_terms, spots_x[2], 0), name, right),
            lax.ppermute(pick(qkv_terms, spots_x[1], 0), name, left),
            lax.ppermute(pick(qkv_terms, spots_x[3], 0), name, across(RING_X)),
        ],
        spots_x,
        0,
    ).astype(f32)
    bare = [
        qkv_grad[..., low_end:high_end].transpose(1, 0, 2).reshape(rows, -1)
        for low_end, high_end in ((0, WIDE), (WIDE, WIDE + HEAD), (WIDE + HEAD, PACK))
    ]
    gain_two_grad = jnp.sum(qkv_grad[..., PACK], 0)
    gain_one_grad = sum(jnp.sum(w * b, 1) for w, b in zip(low, bare))
    grads = [b * gain_one for b in bare]
    grads += [output_grad, mlp_grads[0], mlp_grads[1], mlp_grads[2]]
    grads.append(jnp.stack([gain_one_grad, gain_two_grad], 1))

    outputs = [hidden_out[None], hidden_grad[None]]
    for kind in range(8):
        full = grads[kind][None]
        outputs.append(full)
        outputs.extend(
            adam_step(
                weights[kind], firsts[kind], seconds[kind], full, RATES[kind], DECAYS[kind]
            )
        )
    return tuple(outputs)


def solution(mesh):
    by_axis = jax.sharding.Mesh(mesh.devices.reshape(4, 2, 2, 4, 2), AXES)
    along_ctx, along_fsdp = ("x", "zl"), ("zh", "y", "core")
    by_token = P(along_fsdp, along_ctx, None)
    by_row = P(None, AXES, None)
    return jax.shard_map(
        body,
        mesh=by_axis,
        in_specs=(by_token, by_token, P(along_fsdp, None), P(along_fsdp, along_ctx))
        + (by_row,) * 24,
        out_specs=(by_token, by_token) + (by_row,) * 32,
        check_vma=False,
    )
```

```python
import functools
import math

import jax
import jax.numpy as jnp
from jax import lax
from jax.experimental import pallas as pl
from jax.experimental.pallas import tpu as pltpu
from jax.sharding import PartitionSpec as P

D = 2048
HEADS = 32
KV_HEADS = 4
HEAD = 64
FF = 5632
STEP = 10
N_CTX = 8
N_X = 4
MINE = HEADS // N_X
WIDE = MINE * HEAD
PACK = WIDE + 2 * HEAD
UNITS = 44
PADDED = 48

EPS = 1e-05
NEG = -1e30
BETA_ONE = 0.9
BETA_TWO = 0.95
ADAM_EPS = 1e-08
RATES = (0.1, 0.1, 0.1, 1.5, 0.1, 0.1, 0.066, 0.5)
DECAYS = (0.1, 0.1, 0.1, 0.1, 0.1, 0.1, 0.1, 0.0)
BY_COLUMN = (((1,), (1,)), ((), ()))
BY_ROW = (((0,), (0,)), ((), ()))
bf16 = jnp.bfloat16
f32 = jnp.float32

AXES = ("x", "zl", "zh", "y", "core")
SHARE = ("zh", "zl", "y")
SWAP = [(0, 1), (1, 0)]
RING_X = ("x", [(i, (i + 1) % 4) for i in range(4)], [(i, (i - 1) % 4) for i in range(4)])
RING_Y = ("y",) + RING_X[1:]
DEPTH = (0, 2, 1, 3)
RING_Z = (
    ("zl", "zh"),
    [(DEPTH[i], DEPTH[(i + 1) % 4]) for i in range(4)],
    [(DEPTH[i], DEPTH[(i - 1) % 4]) for i in range(4)],
)
STEPS = (0, -1, 1, 2)


def across(ring):
    there = dict(ring[1])
    return [(i, there[there[i]]) for i in there]


def after(value, *others):
    return lax.optimization_barrier((value,) + others)[0]


def after_all(values, *others):
    return list(lax.optimization_barrier(tuple(values) + others)[: len(values)])


def tick(value):
    return lax.ppermute(value[:16, :128], "core", SWAP)


def add(*terms):
    total = terms[0].astype(f32)
    for term in terms[1:]:
        total = total + term.astype(f32)
    return total


def ring_sides(block, ring):
    name, right, left = ring
    return [lax.ppermute(block, name, right), lax.ppermute(block, name, left)]


def ring_far(sides, ring):
    name, right, left = ring
    half = sides[0].shape[0] // 2
    return [
        lax.ppermute(sides[0][:half], name, right),
        lax.ppermute(sides[1][half:], name, left),
    ]


def ring_halves(block, ring):
    sides = ring_sides(block, ring)
    return [block] + sides + ring_far(sides, ring)


def ring_small(block, ring):
    name, right, left = ring
    return [
        block,
        lax.ppermute(block, name, right),
        lax.ppermute(block, name, left),
        lax.ppermute(block, name, across(ring)),
    ]


def ring_sum_small(own, to_left, to_right, far, ring):
    name, right, left = ring
    return add(
        own,
        lax.ppermute(to_left, name, left),
        lax.ppermute(to_right, name, right),
        lax.ppermute(far, name, across(ring)),
    )


def ring_spots():
    at = lax.axis_index("x"), lax.axis_index("y")
    side, far_side, core = (lax.axis_index(n) for n in ("zl", "zh", "core"))
    spots_x, spots_y = ([(a + step) % 4 for step in STEPS] for a in at)
    depth = [(far_side * 2 + side + step) % 4 for step in STEPS]
    spots_z = [d % 2 * 2 + d // 2 for d in depth]
    return spots_x, spots_y, spots_z, [core, 1 - core]


def pick(value, spot, axis):
    return lax.dynamic_index_in_dim(value, spot, axis, False)


def rope_tables(places):
    half = HEAD // 2
    freqs = jnp.exp(jnp.arange(half, dtype=f32) * (-2.0 * math.log(10000.0) / HEAD))
    angles = places.astype(f32)[:, None] * freqs[None, :]
    return jnp.cos(angles), jnp.sin(angles)


def adam_step(weight, first, second, grad, rate, decay):
    momentum = BETA_ONE * first + (1.0 - BETA_ONE) * grad
    variance = BETA_TWO * second + (1.0 - BETA_TWO) * grad * grad
    corrected = momentum / (1.0 - BETA_ONE**STEP)
    root = jnp.sqrt(variance / (1.0 - BETA_TWO**STEP))
    update = weight - rate * (corrected / (root + ADAM_EPS) + decay * weight)
    return (update, momentum, variance)


def call(kernel, outs, ins, scratch=(), prefetch=(), flops=0, traffic=0, room=16):
    spec_any = pl.BlockSpec(memory_space=pl.ANY)
    spec_vmem = pl.BlockSpec(memory_space=pltpu.VMEM)
    spec_smem = pl.BlockSpec(memory_space=pltpu.SMEM)
    return pl.pallas_call(
        kernel,
        out_shape=[jax.ShapeDtypeStruct(shape, kind) for shape, kind in outs],
        in_specs=[spec_smem] * len(prefetch)
        + [spec_vmem if inside else spec_any for _, inside in ins],
        out_specs=[spec_vmem] * len(outs),
        scratch_shapes=list(scratch),
        compiler_params=pltpu.CompilerParams(vmem_limit_bytes=room * 2**20),
        cost_estimate=pl.CostEstimate(
            flops=flops // 1000, bytes_accessed=traffic // 1000, transcendentals=0
        ),
    )(*prefetch, *(array for array, _ in ins))


def matmul(left, right, dims=(((1,), (0,)), ((), ()))):
    return lax.dot_general(left, right, dims, preferred_element_type=f32)


def lanes(shape):
    return lax.broadcasted_iota(jnp.int32, shape, 1)


def prepare_kernel(state_ref, table_ref, out_ref):
    value = state_ref[...].astype(f32)
    scale = lax.rsqrt(jnp.mean(value * value, -1, keepdims=True) + EPS)
    out_ref[:, :D] = (value * scale).astype(bf16)
    out_ref[:, D:] = table_ref[...]


def join_kernel(*refs):
    at = 0
    for ref in refs[:-1]:
        refs[-1][at : at + ref.shape[0], :] = ref[...]
        at += ref.shape[0]


def join_weights_kernel(own_ref, left_ref, right_ref, far_ref, output_ref, out_ref):
    for i, ref in enumerate((own_ref, left_ref, right_ref, far_ref)):
        rows = slice(i * 16, i * 16 + 16)
        out_ref[rows, : PACK + 128] = ref[...]
        out_ref[rows, PACK + 128 :] = output_ref[:, i * 512 : i * 512 + 512]


def join(blocks):
    shape = (sum(b.shape[0] for b in blocks), blocks[0].shape[1])
    return call(join_kernel, [(shape, blocks[0].dtype)], [(b, True) for b in blocks])[0]


def swap_halves(value):
    low = lanes(value.shape) % HEAD < HEAD // 2
    return jnp.where(low, pltpu.roll(value, 96, 1), pltpu.roll(value, 32, 1))


def rope_factors(angles):
    low = lanes(angles.shape) % HEAD < HEAD // 2
    cosine = jnp.where(low, angles, pltpu.roll(angles, 32, 1))
    sine = jnp.where(low, -pltpu.roll(angles, 96, 1), angles)
    return cosine, sine


PIECES = (128, 128, 128, 64, 64)


def starts(sizes):
    at, found = 0, []
    for size in sizes:
        found.append(at)
        at += size
    return found


def project_kernel(spots, *refs):
    tokens, weights = refs[:5], refs[5:15]
    query_ref, pair_ref, normed_ref, full_ref, gain_ref, angle_ref, output_ref = refs[15:22]
    table_buf = refs[22]
    for at, token in zip(starts(PIECES), tokens):
        rows = slice(at, at + token.shape[0])
        normed_ref[rows, :] = token[:, :D]
        table_buf[rows, :] = token[:, D:]
    for side in range(2):
        for deep in range(4):
            for up in range(4):
                for along in range(4):
                    at = up * 64 + along * 16
                    piece = weights[side * 5 + deep]
                    if deep == 3 and up > 1:
                        at, piece = at - 128, weights[side * 5 + 4]
                    block = piece[at : at + 16, :]
                    to = spots[along] * 4 + spots[8 + deep]
                    to = ((to * 4 + spots[4 + up]) * 2 + spots[12 + side]) * 16
                    to = pl.multiple_of(to, 16)
                    full_ref[pl.ds(to, 16), :] = block[:, :PACK]
                    gain_ref[pl.ds(to, 16), :] = block[:, PACK : PACK + 128]
                    to = (spots[8 + deep] * 4 + spots[4 + up]) * 2 + spots[12 + side]
                    to = pl.multiple_of(to * 16, 16)
                    cols = slice(along * 512, along * 512 + 512)
                    output_ref[pl.ds(to, 16), cols] = block[:, PACK + 128 :]
    table = table_buf[...].astype(f32)
    angles = table + pltpu.roll(table, 64, 1)
    angle_ref[...] = angles
    for at in range(0, 512, 256):
        rows = slice(at, at + 256)
        cosine, sine = rope_factors(angles[rows])
        for col in range(0, PACK, 128):
            part = matmul(normed_ref[rows, :], full_ref[:, col : col + 128])
            turned = part * cosine + swap_halves(part) * sine
            if col < WIDE:
                query_ref[rows, col : col + 128] = (turned * HEAD**-0.5).astype(bf16)
            else:
                turned = jnp.where(lanes(part.shape) < HEAD, turned, part)
                pair_ref[rows, :] = turned.astype(bf16)


def attend_kernel(query_ref, own_ref, other_ref, row_ref, column_ref, mixed_ref, sum_ref,
                  key_buf, value_buf):
    split_pairs(own_ref, other_ref, key_buf, value_buf)
    visible = column_ref[...] <= row_ref[...]
    logs = jnp.zeros((512, 128), f32)
    for pair in range(MINE // 2):
        cols = slice(pair * 128, pair * 128 + 128)
        both = query_ref[:, cols]
        mixed = jnp.zeros((512, 128), f32)
        for side in range(2):
            scores = matmul(both, key_buf[side], BY_COLUMN)
            scores = jnp.where(visible, scores, NEG)
            peak = jnp.max(scores, -1, keepdims=True)
            expo = jnp.exp(scores - peak)
            total = jnp.sum(expo, -1, keepdims=True)
            probs = (expo * (1.0 / total)).astype(bf16)
            mixed = mixed + matmul(probs, value_buf[side])
            logs = jnp.where(
                lanes(logs.shape) == pair * 2 + side, peak + jnp.log(total), logs
            )
        mixed_ref[:, cols] = mixed.astype(bf16)
    sum_ref[...] = jnp.transpose(logs)


def output_project_kernel(mixed_ref, full_ref, *outs):
    put_parts(
        lambda at, size: matmul(mixed_ref[at : at + size, :], full_ref[...]).astype(bf16), outs
    )


def split_pairs(own_ref, other_ref, key_buf, value_buf):
    for i, ref in enumerate((own_ref, other_ref)):
        rows = slice(i * 512, i * 512 + 512)
        pair = ref[...].astype(f32)
        low = lanes(pair.shape) < HEAD
        key, value = jnp.where(low, pair, 0.0), jnp.where(low, 0.0, pair)
        key_buf[0, rows, :] = key.astype(bf16)
        key_buf[1, rows, :] = pltpu.roll(key, HEAD, 1).astype(bf16)
        value_buf[0, rows, :] = pltpu.roll(value, HEAD, 1).astype(bf16)
        value_buf[1, rows, :] = value.astype(bf16)


def put_parts(rows_at, outs):
    own, left, right, low, high = outs
    value = rows_at(0, 256)
    own[...] = value[:128]
    low[...] = value[128:192]
    left[64:, :] = value[192:]
    value = rows_at(256, 256)
    right[64:, :] = value[:64]
    high[...] = value[64:128]
    left[:64, :] = value[128:192]
    right[:64, :] = value[192:]


def put_both(rows_at, outs):
    first, second = outs[5:]
    put_parts(rows_at, outs[:5])
    put_parts(
        lambda at, size: rows_at(512 + at, size),
        (
            second.at[pl.ds(0, 128)],
            first.at[pl.ds(0, 128)],
            first.at[pl.ds(128, 128)],
            second.at[pl.ds(128, 64)],
            second.at[pl.ds(192, 64)],
        ),
    )


PARTS = (((128, D), bf16), ((128, D), bf16), ((128, D), bf16), ((64, D), bf16), ((64, D), bf16))


def scatter_first(parts):
    name, to_right, to_left = RING_X
    return lax.ppermute(parts[1], name, to_left), lax.ppermute(parts[2], name, to_right)


def scatter_sums(parts, got_left, got_right):
    low = add(parts[3], got_left[:64]).astype(bf16)
    high = add(parts[4], got_right[:64]).astype(bf16)
    return low, high


def scatter_last(parts, got_left, got_right, sums=None):
    name, to_right, to_left = RING_X
    low, high = sums or scatter_sums(parts, got_left, got_right)
    low, high = lax.ppermute(low, name, to_left), lax.ppermute(high, name, to_right)
    return parts[0], got_left, got_right, low, high


def scatter_parts(parts):
    return scatter_last(parts, *scatter_first(parts))


BOTH_PARTS = PARTS + (((256, D), bf16), ((256, D), bf16))


def sum_both(parts, first, second):
    own, left, right, low, high = parts[:5]
    return [
        add(own, second[:128]).astype(bf16),
        add(left, first[:128]).astype(bf16),
        add(right, first[128:]).astype(bf16),
        add(low, second[128:192]).astype(bf16),
        add(high, second[192:]).astype(bf16),
    ]


def sum_arrived(own, got_left, got_right, low, high):
    first = own[:64, :].astype(f32) + got_right[64:, :].astype(f32) + low[...].astype(f32)
    second = own[64:, :].astype(f32) + got_left[64:, :].astype(f32) + high[...].astype(f32)
    return first, second


def residual_kernel(state_ref, gain_ref, own, left, right, low, high, out_ref, rows_ref):
    for at, part in zip((0, 64), sum_arrived(own, left, right, low, high)):
        rows = slice(at, at + 64)
        value = state_ref[rows, :].astype(f32) + part
        out_ref[rows, :] = value
        scale = lax.rsqrt(jnp.mean(value * value, -1, keepdims=True) + EPS)
        rows_ref[rows, :] = (value * scale * gain_ref[...]).astype(bf16)


def back_two_kernel(grad_ref, gain_ref, res_ref, own, left, right, low, high, out_ref, low_ref, term_ref):
    terms = jnp.zeros((1, D), f32)
    for at, part in zip((0, 64), sum_arrived(own, left, right, low, high)):
        rows = slice(at, at + 64)
        value = res_ref[rows, :]
        scale = lax.rsqrt(jnp.mean(value * value, -1, keepdims=True) + EPS)
        normed = value * scale
        terms = terms + jnp.sum(part * normed, 0, keepdims=True)
        weighted = part * gain_ref[...]
        through = scale * (weighted - normed * jnp.mean(weighted * normed, -1, keepdims=True))
        total = grad_ref[rows, :].astype(f32) + through
        out_ref[rows, :] = total
        low_ref[rows, :] = total.astype(bf16)
    term_ref[...] = terms


def output_kernel(grad_ref, state_ref, res_ref, branch_own, own, left, right, low, high,
                  grad_out, hidden_out):
    def half(i):
        return [r.at[pl.ds(i * r.shape[0] // 2, r.shape[0] // 2)] for r in (left, right, low, high)]

    for at, part in zip((0, 64), sum_arrived(own, *half(0))):
        rows = slice(at, at + 64)
        value = state_ref[rows, :].astype(f32)
        scale = lax.rsqrt(jnp.mean(value * value, -1, keepdims=True) + EPS)
        normed = value * scale
        through = scale * (part - normed * jnp.mean(part * normed, -1, keepdims=True))
        grad_out[rows, :] = grad_ref[rows, :] + through
    for at, part in zip((0, 64), sum_arrived(branch_own, *half(1))):
        rows = slice(at, at + 64)
        hidden_out[rows, :] = (res_ref[rows, :] + part).astype(bf16)


def mlp_down_kernel(*refs):
    grads, weight_ref, dhidden_ref, grads_ref, weight_buf, sems = refs[:10], *refs[10:]
    copies = [
        pltpu.make_async_copy(
            weight_ref.at[:, pl.ds(2 * PADDED, PADDED)], weight_buf, sems.at[10]
        )
    ]
    for i, at in enumerate(starts(PIECES + PIECES)):
        target = grads_ref.at[pl.ds(at, grads[i].shape[0])]
        copies.append(pltpu.make_async_copy(grads[i], target, sems.at[i]))
    for copy in copies:
        copy.start()
    for copy in copies:
        copy.wait()
    down = weight_buf[...].reshape(768, D)
    for at in range(0, 1024, 256):
        rows = slice(at, at + 256)
        dhidden_ref[rows, :] = matmul(grads_ref[rows, :], down, BY_COLUMN).astype(bf16)


def lay(pieces, ref, at):
    for start, piece in zip(starts(PIECES + PIECES), pieces):
        if at <= start < at + 256:
            ref[start : start + piece.shape[0], :] = piece[...]


def mlp_kernel(*refs):
    tokens, weight_ref, dhidden_ref = refs[:10], refs[10], refs[11]
    outs = refs[12:19]
    hidden_ref, dgate_ref, dup_ref, rows_ref = refs[19:23]
    gate_w, up_w = (
        weight_ref[:, k * PADDED : (k + 1) * PADDED, :].reshape(768, D) for k in range(2)
    )

    def rows_at(at, size):
        lay(tokens, rows_ref, at)
        rows = slice(at, at + size)
        for col in range(0, 768, 384):
            cols = slice(col, col + 384)
            gate = matmul(rows_ref[rows, :], gate_w[cols], BY_COLUMN)
            up_proj = matmul(rows_ref[rows, :], up_w[cols], BY_COLUMN)
            dhidden = dhidden_ref[rows, cols].astype(f32)
            sigmoid = 1.0 / (1.0 + jnp.exp(-gate))
            silu_gate = gate * sigmoid
            hidden_ref[rows, cols] = (silu_gate * up_proj).astype(bf16)
            slope = sigmoid * (1.0 + gate * (1.0 - sigmoid))
            dgate_ref[rows, cols] = (dhidden * up_proj * slope).astype(bf16)
            dup_ref[rows, cols] = (dhidden * silu_gate).astype(bf16)
        summed = matmul(dgate_ref[rows, :], gate_w) + matmul(dup_ref[rows, :], up_w)
        return summed.astype(bf16)

    put_both(rows_at, outs)


def mlp_grad_kernel(kind, left_ref, right_ref, *refs):
    out_ref, term_buf, sems = refs[-3:]
    width = 512
    copies = []
    for i in range(D // width):
        cols = slice(i * width, (i + 1) * width)
        if i > 1:
            copies[i - 2].wait()
        terms = matmul(left_ref[...], right_ref[:, cols], BY_ROW).astype(bf16)
        term_buf[i % 2] = terms.reshape(16, PADDED, width)
        target = out_ref.at[:, pl.ds(kind * PADDED, PADDED), pl.ds(i * width, width)]
        copies.append(pltpu.make_async_copy(term_buf.at[i % 2], target, sems.at[i]))
        copies[i].start()
    for copy in copies[-2:]:
        copy.wait()


def mlp_grad(kind, left, right, before):
    held = [] if before is None else [before]
    outside = pl.BlockSpec(memory_space=pl.ANY)
    return pl.pallas_call(
        functools.partial(mlp_grad_kernel, kind),
        out_shape=jax.ShapeDtypeStruct((16, 3 * PADDED, D), bf16),
        in_specs=[pl.BlockSpec(memory_space=pltpu.VMEM)] * 2 + [outside] * len(held),
        out_specs=outside,
        scratch_shapes=[
            pltpu.VMEM((2, 16, PADDED, 512), bf16),
            pltpu.SemaphoreType.DMA((D // 512,)),
        ],
        input_output_aliases={2: 0} if held else {},
        compiler_params=pltpu.CompilerParams(vmem_limit_bytes=16 * 2**20),
        cost_estimate=pl.CostEstimate(
            flops=2 * 1024 * 768 * 2, bytes_accessed=8 * 2**10, transcendentals=0
        ),
    )(left, right, *held)


def branch_kernel(hidden_ref, weight_ref, *outs):
    down = weight_ref[:, 2 * PADDED :, :].reshape(768, D)
    put_both(
        lambda at, size: matmul(hidden_ref[at : at + size, :], down).astype(bf16), outs
    )


def unmix_kernel(spots, *refs):
    pieces, full_ref, mixed_ref = refs[:5], refs[5], refs[6]
    dmixed_ref, kept_ref, given_ref, joined_ref, term_buf = refs[7:]
    for at in range(0, 512, 256):
        lay(pieces, joined_ref, at)
        dmixed_ref[at : at + 256, :] = matmul(
            joined_ref[at : at + 256, :], full_ref[...], BY_COLUMN
        ).astype(bf16)
    for at in range(0, 512, 128):
        terms = matmul(mixed_ref[:, at : at + 128], joined_ref[...], BY_ROW).astype(bf16)
        term_buf[at // 32 : at // 32 + 4] = terms.reshape(4, 2, 16, D)
    kept_ref[...] = term_buf[:, spots[12]]
    given_ref[...] = term_buf[:, spots[13]]


def attend_back_kernel(pairs, query_ref, own_ref, other_ref, row_ref, column_ref, sum_ref,
                       mixed_ref, dmixed_ref, angle_ref, *refs):
    before = refs[0] if pairs[0] else None
    dquery_ref, dpair_ref, key_buf, value_buf = refs[1 if pairs[0] else 0 :]
    split_pairs(own_ref, other_ref, key_buf, value_buf)
    turned_keys = [jnp.transpose(key_buf[side].astype(f32)).astype(bf16) for side in range(2)]
    visible = column_ref[...] <= row_ref[...]
    cosine, sine = rope_factors(angle_ref[...])
    low = lanes((1024, 128)) < HEAD
    total = before[...] if pairs[0] else jnp.zeros((1024, 128), f32)
    picks = lax.broadcasted_iota(jnp.int32, (8, 128), 0)
    picks = jnp.where(lanes((8, 128)) // HEAD == picks, 1.0, 0.0)
    for pair in pairs:
        cols = slice(pair * 128, pair * 128 + 128)
        both, dboth = query_ref[:, cols], dmixed_ref[:, cols]
        product = dboth.astype(f32) * mixed_ref[:, cols].astype(f32)
        deltas = lax.dot_general(
            picks, product, BY_COLUMN, precision=lax.Precision.HIGHEST, preferred_element_type=f32
        )
        dquery = jnp.zeros((128, 512), f32)
        dkeys, dvalues = [], []
        for side in range(2):
            head = pair * 2 + side
            scores = matmul(key_buf[side], both, BY_COLUMN)
            probs = jnp.exp(jnp.where(visible, scores, NEG) - sum_ref[head : head + 1, :])
            dprobs = matmul(value_buf[side], dboth, BY_COLUMN)
            dscores = (probs * (dprobs - deltas[side : side + 1, :])).astype(bf16)
            dquery = dquery + matmul(turned_keys[side], dscores)
            dkeys.append(matmul(dscores, both))
            dvalues.append(matmul(probs.astype(bf16), dboth))
        dquery = jnp.transpose(dquery) * HEAD**-0.5
        at = (pair - pairs[0]) * 128
        dquery_ref[:, at : at + 128] = (dquery * cosine - swap_halves(dquery) * sine).astype(bf16)
        dkey = dkeys[0] + pltpu.roll(dkeys[1], HEAD, 1)
        dvalue = pltpu.roll(dvalues[0], HEAD, 1) + dvalues[1]
        total = total + jnp.where(low, dkey, dvalue)
    dpair_ref[...] = total


def query_terms_kernel(normed_ref, first_ref, second_ref, out_ref):
    for at in range(0, D, 512):
        rows = slice(at, at + 512)
        for i, ref in enumerate((first_ref, second_ref)):
            out_ref[rows, i * 256 : i * 256 + 256] = matmul(
                normed_ref[:, rows], ref[...], BY_ROW
            ).astype(bf16)


def terms_kernel(spots, normed_ref, query_ref, gain_ref, dpair_ref, got_ref, angle_ref,
                 pair_ref, kept_ref, given_ref, term_buf):
    total = dpair_ref[:512, :] + got_ref[...].astype(f32)
    cosine, sine = rope_factors(angle_ref[...])
    turned = total * cosine - swap_halves(total) * sine
    total = jnp.where(lanes(total.shape) < HEAD, turned, total)
    pair_ref[...] = total.astype(bf16)
    for at in range(0, D, 512):
        rows, to = slice(at, at + 512), slice(at // 32, at // 32 + 16)
        terms = matmul(normed_ref[:, rows], pair_ref[...], BY_ROW).astype(bf16)
        term_buf[to, :, :, :WIDE] = query_ref[rows, :].reshape(16, 2, 16, WIDE)
        term_buf[to, :, :, WIDE:PACK] = terms.reshape(16, 2, 16, 128)
        term_buf[to, :, :, PACK:] = gain_ref[rows, :].reshape(16, 2, 16, 128)
    kept_ref[...] = term_buf[:, spots[12]]
    given_ref[...] = term_buf[:, spots[13]]


def finish_kernel(first_ref, second_ref, pair_ref, full_ref, *refs):
    branch, outs, proj_buf = refs[:4], refs[4:9], refs[9]
    proj_buf[:, :256] = first_ref[...]
    proj_buf[:, 256:WIDE] = second_ref[...]
    proj_buf[:, WIDE:] = pair_ref[...]
    put_parts(
        lambda at, size: matmul(
            proj_buf[at : at + size, :], full_ref[...], BY_COLUMN
        ).astype(bf16),
        [outs[0]] + [ref.at[pl.ds(0, ref.shape[0] // 2)] for ref in outs[1:]],
    )
    for ref, part in zip(outs[1:], branch):
        ref[ref.shape[0] // 2 :, :] = part[...]


def step_refs(kind, grad, weight, first, second, outs):
    update, momentum, variance = adam_step(weight, first, second, grad, RATES[kind], DECAYS[kind])
    for ref, value in zip(outs, (grad, update, momentum, variance)):
        ref[0] = value


def mlp_adam_kernel(term_ref, *refs):
    for i in range(3):
        grad = term_ref[i * PADDED : (i + 1) * PADDED, :].astype(f32)[:UNITS]
        outs = refs[9 + i * 4 : 13 + i * 4]
        for j in range(16):
            outs[0][pl.ds(j, UNITS, stride=16), :] = grad[:, j * 128 : j * 128 + 128]
        grad, weight, first, second = outs[0][...], *(refs[i * 3 + j][...] for j in range(3))
        kind = 4 + i
        values = adam_step(weight, first, second, grad, RATES[kind], DECAYS[kind])
        for ref, value in zip(outs[1:], values):
            ref[...] = value


def attn_adam_kernel(spots, own_ref, left_ref, right_ref, far_ref, gain_ref, *refs):
    row_ref, grad_buf = refs[21], refs[22]
    pieces = [ref[...].astype(f32) for ref in (own_ref, left_ref, right_ref, far_ref)]
    keys, values = jnp.zeros((16, 256), f32), jnp.zeros((16, 256), f32)
    slot = lanes((16, 256)) // HEAD
    low = lanes((16, 128)) < HEAD
    for i, piece in enumerate(pieces):
        at = pl.multiple_of(spots[i] * WIDE, WIDE)
        grad_buf[:, pl.ds(at, WIDE)] = piece[:, :WIDE]
        pair = piece[:, WIDE:PACK]
        turned = pltpu.roll(pair, HEAD, 1)
        key, value = jnp.where(low, pair, turned), jnp.where(low, turned, pair)
        keys = jnp.where(slot == spots[i], jnp.concatenate([key, key], 1), keys)
        values = jnp.where(slot == spots[i], jnp.concatenate([value, value], 1), values)
    rows = jnp.zeros((16, 1), f32)
    for i, bare in enumerate((grad_buf[...], keys, values)):
        weight, first, second = (refs[i * 3 + j][0] for j in range(3))
        rounded = weight.astype(bf16).astype(f32)
        rows = rows + jnp.sum(rounded * bare, -1, keepdims=True)
        step_refs(i, bare * gain_ref[...], weight, first, second, refs[9 + i * 4 : 13 + i * 4])
    gain_two = sum(piece[:, PACK:] for piece in pieces)
    row_ref[...] = jnp.where(lanes((16, 128)) == 0, rows, gain_two)


def body(
    hidden_in,
    cotangent,
    block_table,
    positions,
    query_weight,
    key_weight,
    value_weight,
    output_weight,
    gate_weight,
    up_weight,
    down_weight,
    norm_gains,
    *moments,
):
    weights = (
        query_weight,
        key_weight,
        value_weight,
        output_weight,
        gate_weight,
        up_weight,
        down_weight,
        norm_gains,
    )
    firsts, seconds = moments[:8], moments[8:]
    tokens = hidden_in.shape[1]
    block_rows = tokens // 2
    spots_x, spots_y, spots_z, spots_core = ring_spots()
    at_side = lax.axis_index("zl")
    places = [spot * 2 + (at_side ^ flip) for flip in range(2) for spot in spots_x]
    table = block_table[0].reshape(N_CTX, 2)[jnp.stack(places)].reshape(-1)
    logical = (
        table[:, None] * block_rows + jnp.arange(block_rows, dtype=jnp.int32)[None, :]
    ).reshape(-1)

    mlp_rows = jnp.concatenate(
        [
            jnp.pad(w[0].astype(bf16), ((0, PADDED - UNITS), (0, 0)))
            for w in (gate_weight, up_weight, down_weight)
        ],
        0,
    )
    gains = norm_gains[0].astype(bf16).astype(f32)
    gain_one = gains[:, :1]
    scaled = [
        (w[0].astype(bf16).astype(f32) * gain_one).astype(bf16)
        for w in (query_weight, key_weight, value_weight)
    ]
    rows = scaled[0].shape[0]
    packed = jnp.concatenate(
        [w.reshape(rows, N_X, -1).transpose(1, 0, 2) for w in scaled]
        + [jnp.broadcast_to(gains[:, 1:].astype(bf16), (N_X, rows, 128))],
        -1,
    )
    spots = jnp.stack(spots_x + spots_y + spots_z + spots_core).astype(jnp.int32)
    row, column = logical[:512], logical
    name, right, left = RING_X
    state = hidden_in[0]
    tables = jnp.concatenate(rope_tables(positions[0]), 1)
    tables_low = tables.astype(bf16)
    rest = (tables - tables_low.astype(f32)).astype(bf16)
    sent = call(
        prepare_kernel,
        [((tokens, D + 128), bf16)],
        [(state, True), (jnp.concatenate([tables_low, rest], 1), True)],
    )[0]
    owned = call(
        join_weights_kernel,
        [((4 * rows, PACK + 128 + 512), bf16)],
        [
            (after(pick(packed, spots_x[0], 0), sent), True),
            (lax.ppermute(pick(packed, spots_x[2], 0), name, right), True),
            (lax.ppermute(pick(packed, spots_x[1], 0), name, left), True),
            (lax.ppermute(pick(packed, spots_x[3], 0), name, across(RING_X)), True),
            (output_weight[0].astype(bf16), True),
        ],
    )[0]
    token_sides = ring_sides(after(sent, owned), RING_X)

    owned = join(after_all(ring_small(owned, RING_Y), *token_sides))
    token_far = ring_far(token_sides, RING_X)
    token_pieces = [sent] + token_sides + token_far
    sides = ring_sides(owned, RING_Z)
    orders = [row[:, None], column[None], row[None], column[:, None], spots]
    *sides, row_tall, column_wide, row_wide, column_tall, spots = after_all(
        sides + orders, *token_far
    )
    far = ring_far(sides, RING_Z)
    mlp_full = lax.all_gather(after(mlp_rows, *far), SHARE, axis=0, tiled=True)
    mlp_full = mlp_full.reshape(-1, 3 * PADDED, D)
    grad_own = after(cotangent[0], *token_far)
    grad_sides = ring_sides(grad_own, RING_X)
    weight_pieces = [owned] + sides + far
    weight_pieces = weight_pieces + [lax.ppermute(b, "core", SWAP) for b in weight_pieces]
    weight_pieces[0] = after(weight_pieces[0], tick(grad_own))
    query, own_pair, normed_all, qkv_full, gain_rows, angles, output_full = call(
        project_kernel,
        [
            ((512, WIDE), bf16),
            ((512, 128), bf16),
            ((512, D), bf16),
            ((D, PACK), bf16),
            ((D, 128), bf16),
            ((512, 128), f32),
            ((WIDE, D), bf16),
        ],
        [(v, True) for v in token_pieces + weight_pieces],
        scratch=[pltpu.VMEM((512, 128), bf16)],
        prefetch=[spots],
        flops=2 * 512 * D * PACK,
        traffic=16 * 2**20,
    )
    gain_two = gain_rows[:, 0].astype(f32)[None]
    other_pair = lax.ppermute(own_pair, "zl", SWAP)
    grad_far = ring_far(after_all(grad_sides, tick(own_pair)), RING_X)
    other_pair = after(other_pair, *grad_far)

    mixed, logs = call(
        attend_kernel,
        [((512, WIDE), bf16), ((128, 512), f32)],
        [(v, True) for v in (query, own_pair, other_pair, row_tall, column_wide)],
        scratch=[pltpu.VMEM((2, 1024, 128), bf16)] * 2,
        flops=4 * 8 * 512 * 1024 * 256,
        traffic=4 * 2**20,
    )
    parts = call(
        output_project_kernel,
        PARTS,
        [(mixed, True), (output_full, True)],
        flops=2 * 512 * D * WIDE,
        traffic=6 * 2**20,
    )
    grad_pieces = [grad_own] + grad_sides + grad_far
    grad_pieces = grad_pieces + [lax.ppermute(b, "core", SWAP) for b in grad_pieces]
    residual, mlp_in = call(
        residual_kernel,
        [((tokens, D), f32), ((tokens, D), bf16)],
        [(v, True) for v in (state, gain_two) + scatter_parts(parts)],
    )

    row_sides = ring_sides(mlp_in, RING_X)
    dhidden, grad_rows = call(
        mlp_down_kernel,
        [((1024, 768), bf16), ((1024, D), bf16)],
        [(v, False) for v in [after(grad_pieces[0], mlp_in)] + grad_pieces[1:] + [mlp_full]],
        scratch=[pltpu.VMEM((16, PADDED, D), bf16), pltpu.SemaphoreType.DMA((11,))],
        flops=2 * 1024 * 768 * D,
        traffic=12 * 2**20,
    )
    row_sides = after_all(row_sides, dhidden)
    row_pieces = [mlp_in] + row_sides + ring_far(row_sides, RING_X)
    row_pieces = row_pieces + [lax.ppermute(b, "core", SWAP) for b in row_pieces]
    *parts, hidden, dgate, dup, rows_in = call(
        mlp_kernel,
        list(BOTH_PARTS) + [((1024, 768), bf16)] * 3 + [((1024, D), bf16)],
        [(v, True) for v in row_pieces + [mlp_full, dhidden]],
        flops=8 * 1024 * 768 * D,
        traffic=26 * 2**20,
    )
    swapped = lax.ppermute(parts[5], "core", SWAP), lax.ppermute(parts[6], "core", SWAP)
    sums = sum_both(parts, *swapped)
    got_left, got_right = scatter_first(sums)
    terms = mlp_grad(0, after(dgate, tick(sums[1])), rows_in, None)
    terms = mlp_grad(1, dup, rows_in, terms)
    second = scatter_sums(sums, got_left, got_right)
    terms = mlp_grad(2, after(hidden, tick(second[0])), grad_rows, terms)
    mlp_terms = lax.psum_scatter(
        terms.reshape(-1, D), SHARE, scatter_dimension=0, tiled=True
    )
    arrived = scatter_last(sums, got_left, got_right, second)
    grad_one, grad_low, gain_terms = call(
        back_two_kernel,
        [((tokens, D), f32), ((tokens, D), bf16), ((1, D), f32)],
        [(v, True) for v in (cotangent[0], gain_two, residual) + arrived],
    )
    grad_one_sides = ring_sides(grad_low, RING_X)
    gain_terms = jnp.broadcast_to(gain_terms.reshape(D, 1), (D, 128)).astype(bf16)
    branch = call(
        branch_kernel,
        BOTH_PARTS,
        [(after(hidden, tick(grad_low)), True), (mlp_full, True)],
        flops=2 * 1024 * 768 * D,
        traffic=8 * 2**20,
    )
    grad_one_sides = after_all(grad_one_sides, *branch)
    grad_one_pieces = [grad_low] + grad_one_sides + ring_far(grad_one_sides, RING_X)
    branch = sum_both(
        branch, lax.ppermute(branch[5], "core", SWAP), lax.ppermute(branch[6], "core", SWAP)
    )

    dmixed, kept, given = call(
        unmix_kernel,
        [((512, WIDE), bf16), ((16, rows, D), bf16), ((16, rows, D), bf16)],
        [(v, True) for v in grad_one_pieces + [output_full, mixed]],
        scratch=[
            pltpu.VMEM((512, D), bf16),
            pltpu.VMEM((16, 2, rows, D), bf16),
        ],
        prefetch=[spots],
        flops=4 * 512 * D * WIDE,
        traffic=10 * 2**20,
    )
    given = lax.ppermute(given, "core", SWAP)

    def attend_back(pairs, query, before):
        return call(
            functools.partial(attend_back_kernel, pairs),
            [((512, 256), bf16), ((1024, 128), f32)],
            [
                (v, True)
                for v in (query, own_pair, other_pair, row_wide, column_tall, logs, mixed)
                + (dmixed, angles)
            ]
            + [(v, True) for v in before],
            scratch=[pltpu.VMEM((2, 1024, 128), bf16)] * 2,
            flops=20 * 2 * 512 * 1024 * 256,
            traffic=4 * 2**20,
        )

    dquery_one, dpair = attend_back((0, 1), query, [])
    given = after(given, dquery_one)
    output_terms = add(kept, given).astype(bf16).reshape(4, 4, rows, D)
    output_terms = ring_sum_small(*(pick(output_terms, spot, 0) for spot in spots_z), RING_Z)
    output_terms = output_terms.astype(bf16)
    dquery_two, dpair = attend_back((2, 3), after(query, given), [dpair])
    dqueries = [dquery_one, dquery_two]
    got = lax.ppermute(dpair[512:].astype(bf16), "zl", SWAP)
    query_terms = call(
        query_terms_kernel,
        [((D, WIDE), bf16)],
        [(v, True) for v in [normed_all] + dqueries],
        flops=2 * 512 * D * WIDE,
        traffic=6 * 2**20,
    )[0]
    dpair_low, kept, given = call(
        terms_kernel,
        [((512, 128), bf16), ((64, rows, PACK + 128), bf16), ((64, rows, PACK + 128), bf16)],
        [
            (v, True)
            for v in (normed_all, query_terms, gain_terms, dpair, got, angles)
        ],
        scratch=[pltpu.VMEM((64, 2, rows, PACK + 128), bf16)],
        prefetch=[spots],
        flops=2 * 512 * D * 256,
        traffic=8 * 2**20,
    )
    given = lax.ppermute(given, "core", SWAP)
    parts = call(
        finish_kernel,
        [((128, D), bf16)] + [((256, D), bf16)] * 2 + [((128, D), bf16)] * 2,
        [(v, True) for v in dqueries + [dpair_low, qkv_full] + branch[1:]],
        scratch=[pltpu.VMEM((512, PACK), bf16)],
        flops=2 * 512 * D * PACK,
        traffic=8 * 2**20,
    )
    qkv_terms = add(kept, given).astype(bf16)
    qkv_terms = qkv_terms.reshape(N_X, 4, 4, rows, -1)
    qkv_terms = ring_sum_small(*(pick(qkv_terms, spot, 1) for spot in spots_z), RING_Z)
    qkv_terms = qkv_terms.astype(bf16)
    got_left, got_right = scatter_first(parts)
    low, high = (
        add(ahead.reshape(2, 64, D), got.reshape(2, 128, D)[:, :64]).astype(bf16).reshape(128, D)
        for ahead, got in ((parts[3], got_left), (parts[4], got_right))
    )
    arrived = scatter_last(parts, got_left, got_right, (low, high))
    hidden_grad, hidden_out = call(
        output_kernel,
        [((tokens, D), f32), ((tokens, D), bf16)],
        [(v, True) for v in (grad_one, state, residual, branch[0]) + arrived],
    )
    def shard(kind):
        return [(v[kind], True) for v in (weights, firsts, seconds)]

    def stepped(kinds):
        return [(weights[kind].shape, f32) for kind in kinds for _ in range(4)]

    mlp_steps = call(
        mlp_adam_kernel,
        [((UNITS * 16, 128), f32)] * 12,
        [(after(mlp_terms, dpair_low), True)]
        + [(v.reshape(UNITS * 16, 128), True) for k in (4, 5, 6) for v, _ in shard(k)],
        traffic=8 * 2**20,
    )
    output_terms = after(output_terms, qkv_terms)
    output_grad = ring_sum_small(*(pick(output_terms, spot, 0) for spot in spots_y), RING_Y)
    qkv_terms = after(qkv_terms, mlp_steps[0], parts[0])
    qkv_terms = ring_sum_small(*(pick(qkv_terms, spot, 1) for spot in spots_y), RING_Y)
    qkv_terms = qkv_terms.astype(bf16)

    *attn_steps, gain_rows = call(
        attn_adam_kernel,
        stepped((0, 1, 2)) + [((rows, 128), f32)],
        [
            (pick(qkv_terms, spots_x[0], 0), True),
            (lax.ppermute(pick(qkv_terms, spots_x[2], 0), name, right), True),
            (lax.ppermute(pick(qkv_terms, spots_x[1], 0), name, left), True),
            (lax.ppermute(pick(qkv_terms, spots_x[3], 0), name, across(RING_X)), True),
            (gain_one, True),
        ]
        + shard(0)
        + shard(1)
        + shard(2),
        scratch=[pltpu.VMEM((rows, D), f32)],
        prefetch=[spots],
        traffic=2 * 2**20,
    )

    def step(kind, grad):
        full = grad[None]
        return [full] + list(
            adam_step(weights[kind], firsts[kind], seconds[kind], full, RATES[kind], DECAYS[kind])
        )

    outputs = [hidden_out[None], hidden_grad[None]]
    outputs += attn_steps + step(3, output_grad)
    outputs += [v.reshape(1, UNITS, D) for v in mlp_steps] + step(7, gain_rows[:, :2])
    return tuple(outputs)


def solution(mesh):
    by_axis = jax.sharding.Mesh(mesh.devices.reshape(4, 2, 2, 4, 2), AXES)
    along_ctx, along_fsdp = ("x", "zl"), ("zh", "y", "core")
    by_token = P(along_fsdp, along_ctx, None)
    by_row = P(None, AXES, None)
    return jax.shard_map(
        body,
        mesh=by_axis,
        in_specs=(by_token, by_token, P(along_fsdp, None), P(along_fsdp, along_ctx))
        + (by_row,) * 24,
        out_specs=(by_token, by_token) + (by_row,) * 32,
        check_vma=False,
    )
```

```python
import functools
import math

import jax
import jax.numpy as jnp
from jax import lax
from jax.experimental import pallas as pl
from jax.experimental.pallas import tpu as pltpu
from jax.sharding import PartitionSpec as P

D = 2048
HEADS = 32
KV_HEADS = 4
HEAD = 64
FF = 5632
STEP = 10
N_CTX = 8
N_X = 4
MINE = HEADS // N_X
WIDE = MINE * HEAD
PACK = WIDE + 2 * HEAD
UNITS = 44
PADDED = 48

EPS = 1e-05
NEG = -1e30
BETA_ONE = 0.9
BETA_TWO = 0.95
ADAM_EPS = 1e-08
RATES = (0.1, 0.1, 0.1, 1.5, 0.1, 0.1, 0.066, 0.5)
DECAYS = (0.1, 0.1, 0.1, 0.1, 0.1, 0.1, 0.1, 0.0)
BY_COLUMN = (((1,), (1,)), ((), ()))
BY_ROW = (((0,), (0,)), ((), ()))
bf16 = jnp.bfloat16
f32 = jnp.float32

AXES = ("x", "zl", "zh", "y", "core")
SHARE = ("zh", "zl", "y")
SWAP = [(0, 1), (1, 0)]
RING_X = ("x", [(i, (i + 1) % 4) for i in range(4)], [(i, (i - 1) % 4) for i in range(4)])
RING_Y = ("y",) + RING_X[1:]
DEPTH = (0, 2, 1, 3)
RING_Z = (
    ("zl", "zh"),
    [(DEPTH[i], DEPTH[(i + 1) % 4]) for i in range(4)],
    [(DEPTH[i], DEPTH[(i - 1) % 4]) for i in range(4)],
)
STEPS = (0, -1, 1, 2)


def across(ring):
    there = dict(ring[1])
    return [(i, there[there[i]]) for i in there]


def after(value, *others):
    return lax.optimization_barrier((value,) + others)[0]


def after_all(values, *others):
    return list(lax.optimization_barrier(tuple(values) + others)[: len(values)])


def tick(value):
    return lax.ppermute(value[:16, :128], "core", SWAP)


def add(*terms):
    total = terms[0].astype(f32)
    for term in terms[1:]:
        total = total + term.astype(f32)
    return total


def ring_sides(block, ring):
    name, right, left = ring
    return [lax.ppermute(block, name, right), lax.ppermute(block, name, left)]


def ring_far(sides, ring):
    name, right, left = ring
    half = sides[0].shape[0] // 2
    return [
        lax.ppermute(sides[0][:half], name, right),
        lax.ppermute(sides[1][half:], name, left),
    ]


def ring_halves(block, ring):
    sides = ring_sides(block, ring)
    return [block] + sides + ring_far(sides, ring)


def ring_small(block, ring):
    name, right, left = ring
    return [
        block,
        lax.ppermute(block, name, right),
        lax.ppermute(block, name, left),
        lax.ppermute(block, name, across(ring)),
    ]


def ring_sum_small(own, to_left, to_right, far, ring):
    name, right, left = ring
    return add(
        own,
        lax.ppermute(to_left, name, left),
        lax.ppermute(to_right, name, right),
        lax.ppermute(far, name, across(ring)),
    )


def ring_spots():
    at = lax.axis_index("x"), lax.axis_index("y")
    side, far_side, core = (lax.axis_index(n) for n in ("zl", "zh", "core"))
    spots_x, spots_y = ([(a + step) % 4 for step in STEPS] for a in at)
    depth = [(far_side * 2 + side + step) % 4 for step in STEPS]
    spots_z = [d % 2 * 2 + d // 2 for d in depth]
    return spots_x, spots_y, spots_z, [core, 1 - core]


def pick(value, spot, axis):
    return lax.dynamic_index_in_dim(value, spot, axis, False)


def rope_tables(places):
    half = HEAD // 2
    freqs = jnp.exp(jnp.arange(half, dtype=f32) * (-2.0 * math.log(10000.0) / HEAD))
    angles = places.astype(f32)[:, None] * freqs[None, :]
    return jnp.cos(angles), jnp.sin(angles)


def adam_step(weight, first, second, grad, rate, decay):
    momentum = BETA_ONE * first + (1.0 - BETA_ONE) * grad
    variance = BETA_TWO * second + (1.0 - BETA_TWO) * grad * grad
    corrected = momentum / (1.0 - BETA_ONE**STEP)
    root = jnp.sqrt(variance / (1.0 - BETA_TWO**STEP))
    update = weight - rate * (corrected / (root + ADAM_EPS) + decay * weight)
    return (update, momentum, variance)


def call(
    kernel, outs, ins, scratch=(), prefetch=(), flops=0, traffic=0, room=16, later=()
):
    read, waits = len(prefetch) + len(ins), len(later)
    ins = list(ins) + [(value, False) for value in later]

    def body(*refs):
        return kernel(*refs[:read], *refs[read + waits :])

    spec_any = pl.BlockSpec(memory_space=pl.ANY)
    spec_vmem = pl.BlockSpec(memory_space=pltpu.VMEM)
    spec_smem = pl.BlockSpec(memory_space=pltpu.SMEM)
    return pl.pallas_call(
        body,
        out_shape=[jax.ShapeDtypeStruct(shape, kind) for shape, kind in outs],
        in_specs=[spec_smem] * len(prefetch)
        + [spec_vmem if inside else spec_any for _, inside in ins],
        out_specs=[spec_vmem] * len(outs),
        scratch_shapes=list(scratch),
        compiler_params=pltpu.CompilerParams(vmem_limit_bytes=room * 2**20),
        cost_estimate=pl.CostEstimate(
            flops=flops // 1000, bytes_accessed=traffic // 1000, transcendentals=0
        ),
    )(*prefetch, *(array for array, _ in ins))


def matmul(left, right, dims=(((1,), (0,)), ((), ()))):
    return lax.dot_general(left, right, dims, preferred_element_type=f32)


def lanes(shape):
    return lax.broadcasted_iota(jnp.int32, shape, 1)


def prepare_kernel(state_ref, table_ref, out_ref):
    value = state_ref[...].astype(f32)
    scale = lax.rsqrt(jnp.mean(value * value, -1, keepdims=True) + EPS)
    out_ref[:, :D] = (value * scale).astype(bf16)
    out_ref[:, D:] = table_ref[...]


def join_kernel(*refs):
    at = 0
    for ref in refs[:-1]:
        refs[-1][at : at + ref.shape[0], :] = ref[...]
        at += ref.shape[0]


def join_weights_kernel(own_ref, left_ref, right_ref, far_ref, output_ref, out_ref):
    for i, ref in enumerate((own_ref, left_ref, right_ref, far_ref)):
        rows = slice(i * 16, i * 16 + 16)
        out_ref[rows, : PACK + 128] = ref[...]
        out_ref[rows, PACK + 128 :] = output_ref[:, i * 512 : i * 512 + 512]


def join(blocks):
    shape = (sum(b.shape[0] for b in blocks), blocks[0].shape[1])
    return call(join_kernel, [(shape, blocks[0].dtype)], [(b, True) for b in blocks])[0]


def swap_halves(value):
    low = lanes(value.shape) % HEAD < HEAD // 2
    return jnp.where(low, pltpu.roll(value, 96, 1), pltpu.roll(value, 32, 1))


def rope_factors(angles):
    low = lanes(angles.shape) % HEAD < HEAD // 2
    cosine = jnp.where(low, angles, pltpu.roll(angles, 32, 1))
    sine = jnp.where(low, -pltpu.roll(angles, 96, 1), angles)
    return cosine, sine


PIECES = (128, 128, 128, 64, 64)


def starts(sizes):
    at, found = 0, []
    for size in sizes:
        found.append(at)
        at += size
    return found


def project_kernel(spots, *refs):
    tokens, weights = refs[:5], refs[5:15]
    query_ref, pair_ref, normed_ref, full_ref, gain_ref, angle_ref, output_ref = refs[15:22]
    table_buf = refs[22]
    for at, token in zip(starts(PIECES), tokens):
        rows = slice(at, at + token.shape[0])
        normed_ref[rows, :] = token[:, :D]
        table_buf[rows, :] = token[:, D:]
    for side in range(2):
        for deep in range(4):
            for up in range(4):
                for along in range(4):
                    at = up * 64 + along * 16
                    piece = weights[side * 5 + deep]
                    if deep == 3 and up > 1:
                        at, piece = at - 128, weights[side * 5 + 4]
                    block = piece[at : at + 16, :]
                    to = spots[along] * 4 + spots[8 + deep]
                    to = ((to * 4 + spots[4 + up]) * 2 + spots[12 + side]) * 16
                    to = pl.multiple_of(to, 16)
                    full_ref[pl.ds(to, 16), :] = block[:, :PACK]
                    gain_ref[pl.ds(to, 16), :] = block[:, PACK : PACK + 128]
                    to = (spots[8 + deep] * 4 + spots[4 + up]) * 2 + spots[12 + side]
                    to = pl.multiple_of(to * 16, 16)
                    cols = slice(along * 512, along * 512 + 512)
                    output_ref[pl.ds(to, 16), cols] = block[:, PACK + 128 :]
    table = table_buf[...].astype(f32)
    angles = table + pltpu.roll(table, 64, 1)
    angle_ref[...] = angles
    for at in range(0, 512, 256):
        rows = slice(at, at + 256)
        cosine, sine = rope_factors(angles[rows])
        for col in range(0, PACK, 128):
            part = matmul(normed_ref[rows, :], full_ref[:, col : col + 128])
            turned = part * cosine + swap_halves(part) * sine
            if col < WIDE:
                query_ref[rows, col : col + 128] = (turned * HEAD**-0.5).astype(bf16)
            else:
                turned = jnp.where(lanes(part.shape) < HEAD, turned, part)
                pair_ref[rows, :] = turned.astype(bf16)


def attend_kernel(query_ref, own_ref, other_ref, row_ref, column_ref, mixed_ref, sum_ref,
                  key_buf, value_buf):
    split_pairs(own_ref, other_ref, key_buf, value_buf)
    visible = column_ref[...] <= row_ref[...]
    logs = jnp.zeros((512, 128), f32)
    for pair in range(MINE // 2):
        cols = slice(pair * 128, pair * 128 + 128)
        both = query_ref[:, cols]
        mixed = jnp.zeros((512, 128), f32)
        for side in range(2):
            scores = matmul(both, key_buf[side], BY_COLUMN)
            scores = jnp.where(visible, scores, NEG)
            peak = jnp.max(scores, -1, keepdims=True)
            expo = jnp.exp(scores - peak)
            total = jnp.sum(expo, -1, keepdims=True)
            probs = (expo * (1.0 / total)).astype(bf16)
            mixed = mixed + matmul(probs, value_buf[side])
            logs = jnp.where(
                lanes(logs.shape) == pair * 2 + side, peak + jnp.log(total), logs
            )
        mixed_ref[:, cols] = mixed.astype(bf16)
    sum_ref[...] = jnp.transpose(logs)


def output_project_kernel(mixed_ref, full_ref, *outs):
    put_parts(
        lambda at, size: matmul(mixed_ref[at : at + size, :], full_ref[...]).astype(bf16), outs
    )


def split_pairs(own_ref, other_ref, key_buf, value_buf):
    for i, ref in enumerate((own_ref, other_ref)):
        rows = slice(i * 512, i * 512 + 512)
        pair = ref[...].astype(f32)
        low = lanes(pair.shape) < HEAD
        key, value = jnp.where(low, pair, 0.0), jnp.where(low, 0.0, pair)
        key_buf[0, rows, :] = key.astype(bf16)
        key_buf[1, rows, :] = pltpu.roll(key, HEAD, 1).astype(bf16)
        value_buf[0, rows, :] = pltpu.roll(value, HEAD, 1).astype(bf16)
        value_buf[1, rows, :] = value.astype(bf16)


def put_parts(rows_at, outs):
    own, left, right, low, high = outs
    value = rows_at(0, 256)
    own[...] = value[:128]
    low[...] = value[128:192]
    left[64:, :] = value[192:]
    value = rows_at(256, 256)
    right[64:, :] = value[:64]
    high[...] = value[64:128]
    left[:64, :] = value[128:192]
    right[:64, :] = value[192:]


def put_both(rows_at, outs):
    first, second = outs[5:]
    put_parts(rows_at, outs[:5])
    put_parts(
        lambda at, size: rows_at(512 + at, size),
        (
            second.at[pl.ds(0, 128)],
            first.at[pl.ds(0, 128)],
            first.at[pl.ds(128, 128)],
            second.at[pl.ds(128, 64)],
            second.at[pl.ds(192, 64)],
        ),
    )


PARTS = (((128, D), bf16), ((128, D), bf16), ((128, D), bf16), ((64, D), bf16), ((64, D), bf16))


def scatter_first(parts):
    name, to_right, to_left = RING_X
    return lax.ppermute(parts[1], name, to_left), lax.ppermute(parts[2], name, to_right)


def scatter_sums(parts, got_left, got_right):
    low = add(parts[3], got_left[:64]).astype(bf16)
    high = add(parts[4], got_right[:64]).astype(bf16)
    return low, high


def scatter_last(parts, got_left, got_right, sums=None):
    name, to_right, to_left = RING_X
    low, high = sums or scatter_sums(parts, got_left, got_right)
    low, high = lax.ppermute(low, name, to_left), lax.ppermute(high, name, to_right)
    return parts[0], got_left, got_right, low, high


def scatter_parts(parts):
    return scatter_last(parts, *scatter_first(parts))


BOTH_PARTS = PARTS + (((256, D), bf16), ((256, D), bf16))


def sum_both(parts, first, second):
    own, left, right, low, high = parts[:5]
    return [
        add(own, second[:128]).astype(bf16),
        add(left, first[:128]).astype(bf16),
        add(right, first[128:]).astype(bf16),
        add(low, second[128:192]).astype(bf16),
        add(high, second[192:]).astype(bf16),
    ]


def sum_arrived(own, got_left, got_right, low, high):
    first = own[:64, :].astype(f32) + got_right[64:, :].astype(f32) + low[...].astype(f32)
    second = own[64:, :].astype(f32) + got_left[64:, :].astype(f32) + high[...].astype(f32)
    return first, second


def residual_kernel(state_ref, gain_ref, own, left, right, low, high, out_ref, rows_ref):
    for at, part in zip((0, 64), sum_arrived(own, left, right, low, high)):
        rows = slice(at, at + 64)
        value = state_ref[rows, :].astype(f32) + part
        out_ref[rows, :] = value
        scale = lax.rsqrt(jnp.mean(value * value, -1, keepdims=True) + EPS)
        rows_ref[rows, :] = (value * scale * gain_ref[...]).astype(bf16)


def back_two_kernel(grad_ref, gain_ref, res_ref, own, left, right, low, high, out_ref, low_ref, term_ref):
    terms = jnp.zeros((1, D), f32)
    for at, part in zip((0, 64), sum_arrived(own, left, right, low, high)):
        rows = slice(at, at + 64)
        value = res_ref[rows, :]
        scale = lax.rsqrt(jnp.mean(value * value, -1, keepdims=True) + EPS)
        normed = value * scale
        terms = terms + jnp.sum(part * normed, 0, keepdims=True)
        weighted = part * gain_ref[...]
        through = scale * (weighted - normed * jnp.mean(weighted * normed, -1, keepdims=True))
        total = grad_ref[rows, :].astype(f32) + through
        out_ref[rows, :] = total
        low_ref[rows, :] = total.astype(bf16)
    term_ref[...] = terms


def output_kernel(grad_ref, state_ref, res_ref, branch_own, own, left, right, low, high,
                  grad_out, hidden_out):
    def half(i):
        return [r.at[pl.ds(i * r.shape[0] // 2, r.shape[0] // 2)] for r in (left, right, low, high)]

    for at, part in zip((0, 64), sum_arrived(own, *half(0))):
        rows = slice(at, at + 64)
        value = state_ref[rows, :].astype(f32)
        scale = lax.rsqrt(jnp.mean(value * value, -1, keepdims=True) + EPS)
        normed = value * scale
        through = scale * (part - normed * jnp.mean(part * normed, -1, keepdims=True))
        grad_out[rows, :] = grad_ref[rows, :] + through
    for at, part in zip((0, 64), sum_arrived(branch_own, *half(1))):
        rows = slice(at, at + 64)
        hidden_out[rows, :] = (res_ref[rows, :] + part).astype(bf16)


def fetch(weight_ref, kind, buf, sem):
    return pltpu.make_async_copy(weight_ref.at[:, pl.ds(kind * PADDED, PADDED)], buf, sem)


def mlp_down_kernel(grads_ref, weight_ref, dhidden_ref, weight_buf, sems):
    copy = fetch(weight_ref, 2, weight_buf, sems.at[0])
    copy.start()
    copy.wait()
    down = weight_buf[...].reshape(768, D)
    for at in range(0, 1024, 256):
        rows = slice(at, at + 256)
        dhidden_ref[rows, :] = matmul(grads_ref[rows, :], down, BY_COLUMN).astype(bf16)


def lay(pieces, ref, at):
    for start, piece in zip(starts(PIECES + PIECES), pieces):
        if at <= start < at + 256:
            ref[start : start + piece.shape[0], :] = piece[...]


def mlp_kernel(*refs):
    tokens, weight_ref, dhidden_ref = refs[:10], refs[10], refs[11]
    outs = refs[12:19]
    hidden_ref, dgate_ref, dup_ref, rows_ref = refs[19:23]
    weight_buf, sems = refs[23:]
    copies = [fetch(weight_ref, k, weight_buf.at[k], sems.at[k]) for k in range(2)]
    for copy in copies:
        copy.start()
    lay(tokens, rows_ref, 0)
    for copy in copies:
        copy.wait()
    gate_w, up_w = (weight_buf[k].reshape(768, D) for k in range(2))

    def rows_at(at, size):
        if at:
            lay(tokens, rows_ref, at)
        rows = slice(at, at + size)
        for col in range(0, 768, 384):
            cols = slice(col, col + 384)
            gate = matmul(rows_ref[rows, :], gate_w[cols], BY_COLUMN)
            up_proj = matmul(rows_ref[rows, :], up_w[cols], BY_COLUMN)
            dhidden = dhidden_ref[rows, cols].astype(f32)
            sigmoid = 1.0 / (1.0 + jnp.exp(-gate))
            silu_gate = gate * sigmoid
            hidden_ref[rows, cols] = (silu_gate * up_proj).astype(bf16)
            slope = sigmoid * (1.0 + gate * (1.0 - sigmoid))
            dgate_ref[rows, cols] = (dhidden * up_proj * slope).astype(bf16)
            dup_ref[rows, cols] = (dhidden * silu_gate).astype(bf16)
        summed = matmul(dgate_ref[rows, :], gate_w) + matmul(dup_ref[rows, :], up_w)
        return summed.astype(bf16)

    put_both(rows_at, outs)


def mlp_grad_kernel(kind, left_ref, right_ref, *refs):
    out_ref, term_buf, sems = refs[-3:]
    width = 512
    copies = []
    for i in range(D // width):
        cols = slice(i * width, (i + 1) * width)
        if i > 1:
            copies[i - 2].wait()
        terms = matmul(left_ref[...], right_ref[:, cols], BY_ROW).astype(bf16)
        term_buf[i % 2] = terms.reshape(16, PADDED, width)
        target = out_ref.at[:, pl.ds(kind * PADDED, PADDED), pl.ds(i * width, width)]
        copies.append(pltpu.make_async_copy(term_buf.at[i % 2], target, sems.at[i]))
        copies[i].start()
    for copy in copies[-2:]:
        copy.wait()


def mlp_grad(kind, left, right, before, later=()):
    held = ([] if before is None else [before]) + list(later)
    outside = pl.BlockSpec(memory_space=pltpu.HBM)
    return pl.pallas_call(
        functools.partial(mlp_grad_kernel, kind),
        out_shape=jax.ShapeDtypeStruct((16, 3 * PADDED, D), bf16),
        in_specs=[pl.BlockSpec(memory_space=pltpu.VMEM)] * 2 + [outside] * len(held),
        out_specs=outside,
        scratch_shapes=[
            pltpu.VMEM((2, 16, PADDED, 512), bf16),
            pltpu.SemaphoreType.DMA((D // 512,)),
        ],
        input_output_aliases={} if before is None else {2: 0},
        compiler_params=pltpu.CompilerParams(vmem_limit_bytes=16 * 2**20),
        cost_estimate=pl.CostEstimate(
            flops=2 * 1024 * 768 * 2, bytes_accessed=8 * 2**10, transcendentals=0
        ),
    )(left, right, *held)


def branch_kernel(hidden_ref, weight_ref, *refs):
    outs, weight_buf, sems = refs[:7], refs[7], refs[8]
    copy = fetch(weight_ref, 2, weight_buf, sems.at[0])
    copy.start()
    copy.wait()
    down = weight_buf[...].reshape(768, D)
    put_both(
        lambda at, size: matmul(hidden_ref[at : at + size, :], down).astype(bf16), outs
    )


def unmix_kernel(spots, *refs):
    pieces, full_ref, mixed_ref = refs[:5], refs[5], refs[6]
    dmixed_ref, kept_ref, given_ref, joined_ref, term_buf = refs[7:]
    for at in range(0, 512, 256):
        lay(pieces, joined_ref, at)
        dmixed_ref[at : at + 256, :] = matmul(
            joined_ref[at : at + 256, :], full_ref[...], BY_COLUMN
        ).astype(bf16)
    for at in range(0, 512, 128):
        terms = matmul(mixed_ref[:, at : at + 128], joined_ref[...], BY_ROW).astype(bf16)
        term_buf[at // 32 : at // 32 + 4] = terms.reshape(4, 2, 16, D)
    kept_ref[...] = term_buf[:, spots[12]]
    given_ref[...] = term_buf[:, spots[13]]


def attend_back_kernel(pairs, query_ref, own_ref, other_ref, row_ref, column_ref, sum_ref,
                       mixed_ref, dmixed_ref, angle_ref, *refs):
    before = refs[0] if pairs[0] else None
    dquery_ref, dpair_ref, key_buf, value_buf = refs[1 if pairs[0] else 0 :]
    split_pairs(own_ref, other_ref, key_buf, value_buf)
    turned_keys = [jnp.transpose(key_buf[side].astype(f32)).astype(bf16) for side in range(2)]
    visible = column_ref[...] <= row_ref[...]
    cosine, sine = rope_factors(angle_ref[...])
    low = lanes((1024, 128)) < HEAD
    total = before[...] if pairs[0] else jnp.zeros((1024, 128), f32)
    picks = lax.broadcasted_iota(jnp.int32, (8, 128), 0)
    picks = jnp.where(lanes((8, 128)) // HEAD == picks, 1.0, 0.0)
    for pair in pairs:
        cols = slice(pair * 128, pair * 128 + 128)
        both, dboth = query_ref[:, cols], dmixed_ref[:, cols]
        product = dboth.astype(f32) * mixed_ref[:, cols].astype(f32)
        deltas = lax.dot_general(
            picks, product, BY_COLUMN, precision=lax.Precision.HIGHEST, preferred_element_type=f32
        )
        dquery = jnp.zeros((128, 512), f32)
        dkeys, dvalues = [], []
        for side in range(2):
            head = pair * 2 + side
            scores = matmul(key_buf[side], both, BY_COLUMN)
            probs = jnp.exp(jnp.where(visible, scores, NEG) - sum_ref[head : head + 1, :])
            dprobs = matmul(value_buf[side], dboth, BY_COLUMN)
            dscores = (probs * (dprobs - deltas[side : side + 1, :])).astype(bf16)
            dquery = dquery + matmul(turned_keys[side], dscores)
            dkeys.append(matmul(dscores, both))
            dvalues.append(matmul(probs.astype(bf16), dboth))
        dquery = jnp.transpose(dquery) * HEAD**-0.5
        at = (pair - pairs[0]) * 128
        dquery_ref[:, at : at + 128] = (dquery * cosine - swap_halves(dquery) * sine).astype(bf16)
        dkey = dkeys[0] + pltpu.roll(dkeys[1], HEAD, 1)
        dvalue = pltpu.roll(dvalues[0], HEAD, 1) + dvalues[1]
        total = total + jnp.where(low, dkey, dvalue)
    dpair_ref[...] = total


def query_terms_kernel(normed_ref, first_ref, second_ref, out_ref):
    for at in range(0, D, 512):
        rows = slice(at, at + 512)
        for i, ref in enumerate((first_ref, second_ref)):
            out_ref[rows, i * 256 : i * 256 + 256] = matmul(
                normed_ref[:, rows], ref[...], BY_ROW
            ).astype(bf16)


def terms_kernel(spots, normed_ref, query_ref, gain_ref, dpair_ref, got_ref, angle_ref,
                 pair_ref, kept_ref, given_ref, term_buf):
    total = dpair_ref[:512, :] + got_ref[...].astype(f32)
    cosine, sine = rope_factors(angle_ref[...])
    turned = total * cosine - swap_halves(total) * sine
    total = jnp.where(lanes(total.shape) < HEAD, turned, total)
    pair_ref[...] = total.astype(bf16)
    for at in range(0, D, 512):
        rows, to = slice(at, at + 512), slice(at // 32, at // 32 + 16)
        terms = matmul(normed_ref[:, rows], pair_ref[...], BY_ROW).astype(bf16)
        term_buf[to, :, :, :WIDE] = query_ref[rows, :].reshape(16, 2, 16, WIDE)
        term_buf[to, :, :, WIDE:PACK] = terms.reshape(16, 2, 16, 128)
        term_buf[to, :, :, PACK:] = gain_ref[rows, :].reshape(16, 2, 16, 128)
    kept_ref[...] = term_buf[:, spots[12]]
    given_ref[...] = term_buf[:, spots[13]]


def finish_kernel(first_ref, second_ref, pair_ref, full_ref, *refs):
    branch, outs, proj_buf = refs[:4], refs[4:9], refs[9]
    proj_buf[:, :256] = first_ref[...]
    proj_buf[:, 256:WIDE] = second_ref[...]
    proj_buf[:, WIDE:] = pair_ref[...]
    put_parts(
        lambda at, size: matmul(
            proj_buf[at : at + size, :], full_ref[...], BY_COLUMN
        ).astype(bf16),
        [outs[0]] + [ref.at[pl.ds(0, ref.shape[0] // 2)] for ref in outs[1:]],
    )
    for ref, part in zip(outs[1:], branch):
        ref[ref.shape[0] // 2 :, :] = part[...]


def step_refs(kind, grad, weight, first, second, outs):
    update, momentum, variance = adam_step(weight, first, second, grad, RATES[kind], DECAYS[kind])
    for ref, value in zip(outs, (grad, update, momentum, variance)):
        ref[0] = value


def mlp_adam_kernel(term_ref, *refs):
    for i in range(3):
        grad = term_ref[i * PADDED : (i + 1) * PADDED, :].astype(f32)[:UNITS]
        outs = refs[9 + i * 4 : 13 + i * 4]
        for j in range(16):
            outs[0][pl.ds(j, UNITS, stride=16), :] = grad[:, j * 128 : j * 128 + 128]
        grad, weight, first, second = outs[0][...], *(refs[i * 3 + j][...] for j in range(3))
        kind = 4 + i
        values = adam_step(weight, first, second, grad, RATES[kind], DECAYS[kind])
        for ref, value in zip(outs[1:], values):
            ref[...] = value


def attn_adam_kernel(spots, own_ref, left_ref, right_ref, far_ref, gain_ref, *refs):
    row_ref, grad_buf = refs[21], refs[22]
    pieces = [ref[...].astype(f32) for ref in (own_ref, left_ref, right_ref, far_ref)]
    keys, values = jnp.zeros((16, 256), f32), jnp.zeros((16, 256), f32)
    slot = lanes((16, 256)) // HEAD
    low = lanes((16, 128)) < HEAD
    for i, piece in enumerate(pieces):
        at = pl.multiple_of(spots[i] * WIDE, WIDE)
        grad_buf[:, pl.ds(at, WIDE)] = piece[:, :WIDE]
        pair = piece[:, WIDE:PACK]
        turned = pltpu.roll(pair, HEAD, 1)
        key, value = jnp.where(low, pair, turned), jnp.where(low, turned, pair)
        keys = jnp.where(slot == spots[i], jnp.concatenate([key, key], 1), keys)
        values = jnp.where(slot == spots[i], jnp.concatenate([value, value], 1), values)
    rows = jnp.zeros((16, 1), f32)
    for i, bare in enumerate((grad_buf[...], keys, values)):
        weight, first, second = (refs[i * 3 + j][0] for j in range(3))
        rounded = weight.astype(bf16).astype(f32)
        rows = rows + jnp.sum(rounded * bare, -1, keepdims=True)
        step_refs(i, bare * gain_ref[...], weight, first, second, refs[9 + i * 4 : 13 + i * 4])
    gain_two = sum(piece[:, PACK:] for piece in pieces)
    row_ref[...] = jnp.where(lanes((16, 128)) == 0, rows, gain_two)


def body(
    hidden_in,
    cotangent,
    block_table,
    positions,
    query_weight,
    key_weight,
    value_weight,
    output_weight,
    gate_weight,
    up_weight,
    down_weight,
    norm_gains,
    *moments,
):
    weights = (
        query_weight,
        key_weight,
        value_weight,
        output_weight,
        gate_weight,
        up_weight,
        down_weight,
        norm_gains,
    )
    firsts, seconds = moments[:8], moments[8:]
    tokens = hidden_in.shape[1]
    block_rows = tokens // 2
    spots_x, spots_y, spots_z, spots_core = ring_spots()
    at_side = lax.axis_index("zl")
    places = [spot * 2 + (at_side ^ flip) for flip in range(2) for spot in spots_x]
    table = block_table[0].reshape(N_CTX, 2)[jnp.stack(places)].reshape(-1)
    logical = (
        table[:, None] * block_rows + jnp.arange(block_rows, dtype=jnp.int32)[None, :]
    ).reshape(-1)

    mlp_rows = jnp.concatenate(
        [
            jnp.pad(w[0].astype(bf16), ((0, PADDED - UNITS), (0, 0)))
            for w in (gate_weight, up_weight, down_weight)
        ],
        0,
    )
    gains = norm_gains[0].astype(bf16).astype(f32)
    gain_one = gains[:, :1]
    scaled = [
        (w[0].astype(bf16).astype(f32) * gain_one).astype(bf16)
        for w in (query_weight, key_weight, value_weight)
    ]
    rows = scaled[0].shape[0]
    packed = jnp.concatenate(
        [w.reshape(rows, N_X, -1).transpose(1, 0, 2) for w in scaled]
        + [jnp.broadcast_to(gains[:, 1:].astype(bf16), (N_X, rows, 128))],
        -1,
    )
    spots = jnp.stack(spots_x + spots_y + spots_z + spots_core).astype(jnp.int32)
    row, column = logical[:512], logical
    name, right, left = RING_X
    state = hidden_in[0]
    tables = jnp.concatenate(rope_tables(positions[0]), 1)
    tables_low = tables.astype(bf16)
    rest = (tables - tables_low.astype(f32)).astype(bf16)
    sent = call(
        prepare_kernel,
        [((tokens, D + 128), bf16)],
        [(state, True), (jnp.concatenate([tables_low, rest], 1), True)],
    )[0]
    owned = call(
        join_weights_kernel,
        [((4 * rows, PACK + 128 + 512), bf16)],
        [
            (after(pick(packed, spots_x[0], 0), sent), True),
            (lax.ppermute(pick(packed, spots_x[2], 0), name, right), True),
            (lax.ppermute(pick(packed, spots_x[1], 0), name, left), True),
            (lax.ppermute(pick(packed, spots_x[3], 0), name, across(RING_X)), True),
            (output_weight[0].astype(bf16), True),
        ],
    )[0]
    token_sides = ring_sides(after(sent, owned), RING_X)

    owned = join(after_all(ring_small(owned, RING_Y), *token_sides))
    token_far = ring_far(token_sides, RING_X)
    token_pieces = [sent] + token_sides + token_far
    sides = ring_sides(owned, RING_Z)
    orders = [row[:, None], column[None], row[None], column[:, None], spots]
    *sides, row_tall, column_wide, row_wide, column_tall, spots = after_all(
        sides + orders, *token_far
    )
    far = ring_far(sides, RING_Z)
    mlp_full = lax.all_gather(after(mlp_rows, *far), SHARE, axis=0, tiled=True)
    mlp_full = mlp_full.reshape(-1, 3 * PADDED, D)
    grad_own = after(cotangent[0], *token_far)
    grad_sides = ring_sides(grad_own, RING_X)
    weight_pieces = [owned] + sides + far
    weight_pieces = weight_pieces + [lax.ppermute(b, "core", SWAP) for b in weight_pieces]
    query, own_pair, normed_all, qkv_full, gain_rows, angles, output_full = call(
        project_kernel,
        [
            ((512, WIDE), bf16),
            ((512, 128), bf16),
            ((512, D), bf16),
            ((D, PACK), bf16),
            ((D, 128), bf16),
            ((512, 128), f32),
            ((WIDE, D), bf16),
        ],
        [(v, True) for v in token_pieces + weight_pieces],
        scratch=[pltpu.VMEM((512, 128), bf16)],
        prefetch=[spots],
        flops=2 * 512 * D * PACK,
        traffic=16 * 2**20,
    )
    gain_two = gain_rows[:, 0].astype(f32)[None]
    other_pair = lax.ppermute(own_pair, "zl", SWAP)
    beat = tick(own_pair)
    grad_far = ring_far(after_all(grad_sides, beat), RING_X)
    other_pair = after(other_pair, *grad_far)

    mixed, logs = call(
        attend_kernel,
        [((512, WIDE), bf16), ((128, 512), f32)],
        [(v, True) for v in (query, own_pair, other_pair, row_tall, column_wide)],
        scratch=[pltpu.VMEM((2, 1024, 128), bf16)] * 2,
        flops=4 * 8 * 512 * 1024 * 256,
        traffic=4 * 2**20,
        later=[beat],
    )
    parts = call(
        output_project_kernel,
        PARTS,
        [(mixed, True), (output_full, True)],
        flops=2 * 512 * D * WIDE,
        traffic=6 * 2**20,
    )
    grad_pieces = [grad_own] + grad_sides + grad_far
    grad_pieces = grad_pieces + [lax.ppermute(b, "core", SWAP) for b in grad_pieces]
    grad_rows = call(
        join_kernel,
        [((1024, D), bf16)],
        [(v, True) for v in grad_pieces],
        later=[tick(parts[1])],
    )[0]
    residual, mlp_in = call(
        residual_kernel,
        [((tokens, D), f32), ((tokens, D), bf16)],
        [(v, True) for v in (state, gain_two) + scatter_parts(parts)],
    )

    row_sides = ring_sides(mlp_in, RING_X)
    dhidden = call(
        mlp_down_kernel,
        [((1024, 768), bf16)],
        [(after(grad_rows, mlp_in), True), (mlp_full, False)],
        scratch=[pltpu.VMEM((16, PADDED, D), bf16), pltpu.SemaphoreType.DMA((1,))],
        flops=2 * 1024 * 768 * D,
        traffic=12 * 2**20,
        later=[tick(mlp_in)],
    )[0]
    row_sides = after_all(row_sides, dhidden)
    row_pieces = [mlp_in] + row_sides + ring_far(row_sides, RING_X)
    row_pieces = row_pieces + [lax.ppermute(b, "core", SWAP) for b in row_pieces]
    *parts, hidden, dgate, dup, rows_in = call(
        mlp_kernel,
        list(BOTH_PARTS) + [((1024, 768), bf16)] * 3 + [((1024, D), bf16)],
        [(v, True) for v in row_pieces] + [(mlp_full, False), (dhidden, True)],
        scratch=[pltpu.VMEM((2, 16, PADDED, D), bf16), pltpu.SemaphoreType.DMA((2,))],
        room=20,
        flops=8 * 1024 * 768 * D,
        traffic=26 * 2**20,
    )
    swapped = lax.ppermute(parts[5], "core", SWAP), lax.ppermute(parts[6], "core", SWAP)
    sums = sum_both(parts, *swapped)
    got_left, got_right = scatter_first(sums)
    terms = mlp_grad(0, after(dgate, sums[1], sums[2]), rows_in, None)
    terms = mlp_grad(1, dup, rows_in, terms)
    second = scatter_sums(sums, got_left, got_right)
    terms = mlp_grad(2, hidden, grad_rows, terms)
    terms = after(terms, got_left, got_right)
    mlp_terms = lax.psum_scatter(
        terms.reshape(-1, D), SHARE, scatter_dimension=0, tiled=True
    )
    arrived = scatter_last(sums, got_left, got_right, second)
    grad_one, grad_low, gain_terms = call(
        back_two_kernel,
        [((tokens, D), f32), ((tokens, D), bf16), ((1, D), f32)],
        [(v, True) for v in (cotangent[0], gain_two, residual) + arrived],
    )
    grad_one_sides = ring_sides(grad_low, RING_X)
    gain_terms = jnp.broadcast_to(gain_terms.reshape(D, 1), (D, 128)).astype(bf16)
    branch = call(
        branch_kernel,
        BOTH_PARTS,
        [(hidden, True), (mlp_full, False)],
        scratch=[pltpu.VMEM((16, PADDED, D), bf16), pltpu.SemaphoreType.DMA((1,))],
        later=[tick(grad_low)],
        flops=2 * 1024 * 768 * D,
        traffic=8 * 2**20,
    )
    grad_one_sides = after_all(grad_one_sides, *branch)
    grad_one_pieces = [grad_low] + grad_one_sides + ring_far(grad_one_sides, RING_X)
    branch = sum_both(
        branch, lax.ppermute(branch[5], "core", SWAP), lax.ppermute(branch[6], "core", SWAP)
    )

    dmixed, kept, given = call(
        unmix_kernel,
        [((512, WIDE), bf16), ((16, rows, D), bf16), ((16, rows, D), bf16)],
        [(v, True) for v in grad_one_pieces + [output_full, mixed]],
        scratch=[
            pltpu.VMEM((512, D), bf16),
            pltpu.VMEM((16, 2, rows, D), bf16),
        ],
        prefetch=[spots],
        flops=4 * 512 * D * WIDE,
        traffic=10 * 2**20,
    )
    given = lax.ppermute(given, "core", SWAP)

    def attend_back(pairs, query, before, later=()):
        return call(
            functools.partial(attend_back_kernel, pairs),
            [((512, 256), bf16), ((1024, 128), f32)],
            [
                (v, True)
                for v in (query, own_pair, other_pair, row_wide, column_tall, logs, mixed)
                + (dmixed, angles)
            ]
            + [(v, True) for v in before],
            scratch=[pltpu.VMEM((2, 1024, 128), bf16)] * 2,
            flops=20 * 2 * 512 * 1024 * 256,
            traffic=4 * 2**20,
            later=later,
        )

    dquery_one, dpair = attend_back((0, 1), query, [])
    given = after(given, dquery_one)
    output_terms = add(kept, given).astype(bf16).reshape(4, 4, rows, D)
    output_terms = ring_sum_small(*(pick(output_terms, spot, 0) for spot in spots_z), RING_Z)
    output_terms = output_terms.astype(bf16)
    dquery_two, dpair = attend_back((2, 3), after(query, given), [dpair])
    dqueries = [dquery_one, dquery_two]
    got = lax.ppermute(dpair[512:].astype(bf16), "zl", SWAP)
    query_terms = call(
        query_terms_kernel,
        [((D, WIDE), bf16)],
        [(v, True) for v in [normed_all] + dqueries],
        flops=2 * 512 * D * WIDE,
        traffic=6 * 2**20,
    )[0]
    dpair_low, kept, given = call(
        terms_kernel,
        [((512, 128), bf16), ((64, rows, PACK + 128), bf16), ((64, rows, PACK + 128), bf16)],
        [
            (v, True)
            for v in (normed_all, query_terms, gain_terms, dpair, got, angles)
        ],
        scratch=[pltpu.VMEM((64, 2, rows, PACK + 128), bf16)],
        prefetch=[spots],
        flops=2 * 512 * D * 256,
        traffic=8 * 2**20,
    )
    given = lax.ppermute(given, "core", SWAP)
    parts = call(
        finish_kernel,
        [((128, D), bf16)] + [((256, D), bf16)] * 2 + [((128, D), bf16)] * 2,
        [(v, True) for v in dqueries + [dpair_low, qkv_full] + branch[1:]],
        scratch=[pltpu.VMEM((512, PACK), bf16)],
        flops=2 * 512 * D * PACK,
        traffic=8 * 2**20,
    )
    qkv_terms = add(kept, given).astype(bf16)
    qkv_terms = qkv_terms.reshape(N_X, 4, 4, rows, -1)
    qkv_terms = ring_sum_small(*(pick(qkv_terms, spot, 1) for spot in spots_z), RING_Z)
    qkv_terms = qkv_terms.astype(bf16)
    got_left, got_right = scatter_first(parts)
    low, high = (
        add(ahead.reshape(2, 64, D), got.reshape(2, 128, D)[:, :64]).astype(bf16).reshape(128, D)
        for ahead, got in ((parts[3], got_left), (parts[4], got_right))
    )
    arrived = scatter_last(parts, got_left, got_right, (low, high))
    hidden_grad, hidden_out = call(
        output_kernel,
        [((tokens, D), f32), ((tokens, D), bf16)],
        [(v, True) for v in (grad_one, state, residual, branch[0]) + arrived],
    )
    def shard(kind):
        return [(v[kind], True) for v in (weights, firsts, seconds)]

    def stepped(kinds):
        return [(weights[kind].shape, f32) for kind in kinds for _ in range(4)]

    mlp_steps = call(
        mlp_adam_kernel,
        [((UNITS * 16, 128), f32)] * 12,
        [(after(mlp_terms, dpair_low), True)]
        + [(v.reshape(UNITS * 16, 128), True) for k in (4, 5, 6) for v, _ in shard(k)],
        traffic=8 * 2**20,
    )
    output_terms = after(output_terms, qkv_terms)
    output_grad = ring_sum_small(*(pick(output_terms, spot, 0) for spot in spots_y), RING_Y)
    qkv_terms = after(qkv_terms, mlp_steps[0], parts[0])
    qkv_terms = ring_sum_small(*(pick(qkv_terms, spot, 1) for spot in spots_y), RING_Y)
    qkv_terms = qkv_terms.astype(bf16)

    *attn_steps, gain_rows = call(
        attn_adam_kernel,
        stepped((0, 1, 2)) + [((rows, 128), f32)],
        [
            (pick(qkv_terms, spots_x[0], 0), True),
            (lax.ppermute(pick(qkv_terms, spots_x[2], 0), name, right), True),
            (lax.ppermute(pick(qkv_terms, spots_x[1], 0), name, left), True),
            (lax.ppermute(pick(qkv_terms, spots_x[3], 0), name, across(RING_X)), True),
            (gain_one, True),
        ]
        + shard(0)
        + shard(1)
        + shard(2),
        scratch=[pltpu.VMEM((rows, D), f32)],
        prefetch=[spots],
        traffic=2 * 2**20,
    )

    def step(kind, grad):
        full = grad[None]
        return [full] + list(
            adam_step(weights[kind], firsts[kind], seconds[kind], full, RATES[kind], DECAYS[kind])
        )

    outputs = [hidden_out[None], hidden_grad[None]]
    outputs += attn_steps + step(3, output_grad)
    outputs += [v.reshape(1, UNITS, D) for v in mlp_steps] + step(7, gain_rows[:, :2])
    return tuple(outputs)


def solution(mesh):
    by_axis = jax.sharding.Mesh(mesh.devices.reshape(4, 2, 2, 4, 2), AXES)
    along_ctx, along_fsdp = ("x", "zl"), ("zh", "y", "core")
    by_token = P(along_fsdp, along_ctx, None)
    by_row = P(None, AXES, None)
    return jax.shard_map(
        body,
        mesh=by_axis,
        in_specs=(by_token, by_token, P(along_fsdp, None), P(along_fsdp, along_ctx))
        + (by_row,) * 24,
        out_specs=(by_token, by_token) + (by_row,) * 32,
        check_vma=False,
    )
```
